512 devices in a mesh: stab: 16 (over z), round: 8 (over y, x_lo), shot: 4 (over x_hi, core).
Axes of the slice: x: 4 (x_hi: 2, x_lo: 2; x = x_hi * 2 + x_lo), y: 4, z: 16, core: 2. Of those that a mesh axis runs over, the one named last changes fastest.
Arguments:
- states_in: bfloat16 [8, 64, 624, 256], P('shot', 'round', 'stab'), parts along dimension 0, may hold values from -6 to 6
- bits: int32 [8, 64, 624], P('shot', 'round', 'stab'), parts along dimension 0, may hold values 0 or 1
- coords: int32 [64, 624], P('round', 'stab'), may hold values from 0 to 624
- coord_table: bfloat16 [625, 256], replicated, may hold values from -8 to 8
- flip_embed: bfloat16 [256], replicated, may hold values from -6 to 6
- gain_attn: bfloat16 [256], replicated, may hold values from 0.25 to 1.75
- w_query: bfloat16 [256, 256], replicated, may hold values from -1 to 1
- w_key: bfloat16 [256, 256], replicated, may hold values from -1 to 1
- w_value: bfloat16 [256, 256], replicated, may hold values from -0.375 to 0.375
- w_out: bfloat16 [256, 256], replicated, may hold values from -0.375 to 0.375
- gain_rec: bfloat16 [256], replicated, may hold values from 0.25 to 1.75
- w_decay: bfloat16 [256, 256], replicated, may hold values from -0.375 to 0.375
- decay_bias: float32 [256], replicated, may hold values from -1 to 6
- w_input: bfloat16 [256, 256], replicated, may hold values from -0.375 to 0.375
- w_rec_out: bfloat16 [256, 256], replicated, may hold values from -0.375 to 0.375
- gain_mlp: bfloat16 [256], replicated, may hold values from 0.25 to 1.75
- w_gate: bfloat16 [256, 1024], replicated, may hold values from -0.375 to 0.375
- w_up: bfloat16 [256, 1024], replicated, may hold values from -0.375 to 0.375
- w_down: bfloat16 [1024, 256], replicated, may hold values from -0.1875 to 0.1875
Outputs:
- states: bfloat16 [8, 64, 624, 256], P('shot', 'round', 'stab'), parts along dimension 0
The draws below stay inside these ranges and needn't reach their ends.
There are 4 independent parts, one for each index of `shot`. The reference program is written for one: setup_inputs(seed, part) draws one part's arguments, and reference() takes and returns one part's arrays. A program takes and returns all parts, laid end to end along the dimension named above; an argument that names none is the same for every part. Nothing has to cross between parts.
All inputs are finite; a program needn't handle non-finite values. No bound on the sum of `bits` on one device may be relied on, other than what follows from the above.
Results may differ from the reference program's by a relative error of at most 0.0065.
Values may be sent and summed in bfloat16 or wider, within the bound.
A program may use at most 128 MiB of HBM per device.

```python
import math
import jax
import jax.numpy as jnp
from jax import lax

D = 256
HD = 32
FF = 1024
S = 624
COORDS = 625
B = 2
R = 64


def aligned_factors(key):
    folded = jax.random.fold_in(key, 9173)
    first_key, second_key = jax.random.split(folded)
    sign_row = jnp.where(jax.random.bernoulli(first_key, 0.5, (D,)), 1.0, -1.0).astype(jnp.float32)
    column_dir = jax.random.truncated_normal(second_key, -3.0, 3.0, (D,), jnp.float32)
    return (sign_row / math.sqrt(D), column_dir)


def drawn_weight(key, salt):
    row_dir, column_dir = aligned_factors(key)
    noise = jax.random.truncated_normal(jax.random.fold_in(key, salt), -4.0, 4.0, (D, D), jnp.float32) / math.sqrt(D)
    return (noise + 0.5 * row_dir[:, None] * column_dir[None, :]).astype(jnp.bfloat16)


def draw_w_query(key, part):
    return drawn_weight(key, 311)


def draw_w_key(key, part):
    return drawn_weight(key, 313)


def draw_coord_table(key, part):
    noise_key = jax.random.fold_in(jax.random.fold_in(key, 523), 0)
    table = jax.random.truncated_normal(noise_key, -6.0, 6.0, (COORDS, D), jnp.float32)
    return table.astype(jnp.bfloat16)


def with_ends(entries, key, least, high):
    longest = entries.shape.index(max(entries.shape))
    spots = []
    for shift in (0, 1):
        where = [jax.random.randint(jax.random.fold_in(key, axis), (), 0, length) for axis, length in enumerate(entries.shape)]
        where[longest] = (where[longest] + shift) % entries.shape[longest]
        spots.append(tuple(where))
    return entries.at[spots[0]].set(least).at[spots[1]].set(high)


def block_levels(own_key, dims, shards, low, high):
    loudness, own = 1.0, jax.random.fold_in(own_key, 6)
    for dim, blocks in shards:
        steps = jnp.exp(jax.random.uniform(jax.random.fold_in(own, dim), (blocks,), jnp.float32, low / len(shards), high / len(shards)))
        loudness = loudness * jnp.repeat(steps, dims[dim] // blocks).reshape([-1 if axis == dim else 1 for axis in range(len(dims))])
    return loudness


def scatter_about(rng, extent, scale, limit, cuts=(), dtype=jnp.bfloat16):
    entries = scale * jax.random.normal(rng, extent, jnp.float32)
    if cuts:
        entries = entries * block_levels(rng, extent, cuts, -0.22, 0.18)
    return jnp.clip(entries, -limit, limit).astype(dtype)


def setup_inputs(seed: int = 0, part: int = 0) -> dict:
    key_of = jax.random.split(jax.random.key(seed), 20)
    part_splits = jax.random.split(jax.random.fold_in(key_of[19], part), 20)
    return {
        "states_in": scatter_about(part_splits[0], (B, R, S, D), 1.0, 6.0, ((1, 8), (2, 16))),
        "bits": with_ends((jax.random.randint(part_splits[1], (B, R, S), 0, 4) < 1).astype(jnp.int32), jax.random.fold_in(part_splits[1], 1), 0, 1),
        "coords": with_ends(jax.random.randint(key_of[2], (R, S), 0, COORDS), jax.random.fold_in(key_of[2], 1), 0, COORDS - 1).astype(jnp.int32),
        "coord_table": draw_coord_table(jax.random.fold_in(key_of[19], 71), part),
        "flip_embed": scatter_about(key_of[4], (D,), 1.0, 6.0),
        "gain_attn": jnp.clip(1.0 + 0.15 * jax.random.normal(key_of[5], (D,), jnp.float32), 0.25, 1.75).astype(jnp.bfloat16),
        "w_query": draw_w_query(jax.random.fold_in(key_of[19], 71), part),
        "w_key": draw_w_key(jax.random.fold_in(key_of[19], 71), part),
        "w_value": scatter_about(key_of[8], (D, D), D ** -0.5, 0.375),
        "w_out": scatter_about(key_of[9], (D, D), D ** -0.5, 0.375),
        "gain_rec": jnp.clip(1.0 + 0.15 * jax.random.normal(key_of[10], (D,), jnp.float32), 0.25, 1.75).astype(jnp.bfloat16),
        "w_decay": scatter_about(key_of[11], (D, D), D ** -0.5, 0.375),
        "decay_bias": jnp.clip(jax.random.uniform(key_of[12], (D,), jnp.float32, -1.0, 6.0), -1.0, 6.0),
        "w_input": scatter_about(key_of[13], (D, D), D ** -0.5, 0.375),
        "w_rec_out": scatter_about(key_of[14], (D, D), D ** -0.5, 0.375),
        "gain_mlp": jnp.clip(1.0 + 0.15 * jax.random.normal(key_of[15], (D,), jnp.float32), 0.25, 1.75).astype(jnp.bfloat16),
        "w_gate": scatter_about(key_of[16], (D, FF), D ** -0.5, 0.375),
        "w_up": scatter_about(key_of[17], (D, FF), D ** -0.5, 0.375),
        "w_down": scatter_about(key_of[18], (FF, D), FF ** -0.5, 0.1875),
    }


def norm_rows(values, gain):
    scale = lax.rsqrt(lax.optimization_barrier(jnp.mean(values * values, axis=-1, keepdims=True)) + 1e-05)
    return (values * scale * gain.astype(jnp.float32)).astype(jnp.bfloat16)

def project(left, right):
    return jnp.dot(left, right, preferred_element_type=jnp.float32)

def reference(states_in, bits, coords, coord_table, flip_embed, gain_attn, w_query, w_key, w_value, w_out, gain_rec, w_decay, decay_bias, w_input, w_rec_out, gain_mlp, w_gate, w_up, w_down):
    base = coord_table[coords].astype(jnp.float32)
    signs = (2 * bits - 1).astype(jnp.float32)[..., None]
    start = states_in.astype(jnp.float32) + base[None] + signs * flip_embed.astype(jnp.float32)
    normed = norm_rows(start, gain_attn)
    shots, rounds, stabs, width = start.shape
    heads = width // HD
    query = project(normed, w_query).astype(jnp.bfloat16).reshape(shots * rounds, stabs, heads, HD)
    keys = project(normed, w_key).astype(jnp.bfloat16).reshape(shots * rounds, stabs, heads, HD)
    values = project(normed, w_value).astype(jnp.bfloat16).reshape(shots * rounds, stabs, heads, HD)

    def attend(items):
        q_one, k_one, v_one = items
        scores = jnp.einsum('qhe,khe->hqk', q_one.astype(jnp.float32), k_one.astype(jnp.float32)) * HD ** (-0.5)
        peak = lax.optimization_barrier(jnp.max(scores, axis=-1, keepdims=True))
        expo = jnp.exp(scores - peak)
        total = lax.optimization_barrier(jnp.sum(expo, axis=-1))
        weights = expo.astype(jnp.bfloat16)
        summed = jnp.einsum('hqk,khe->qhe', weights.astype(jnp.float32), v_one.astype(jnp.float32))
        return (summed / jnp.transpose(total, (1, 0))[..., None]).astype(jnp.bfloat16)
    mixed = lax.map(attend, (query, keys, values)).reshape(shots, rounds, stabs, width)
    after_attn = start + project(mixed, w_out)
    rec_in = norm_rows(after_attn, gain_rec)
    decay = jax.nn.sigmoid(project(rec_in, w_decay) + decay_bias)
    drive = (1.0 - decay) * project(rec_in, w_input)

    def advance(state, inputs):
        state = inputs[0] * state + inputs[1]
        return (state, state)
    _, hidden = lax.scan(advance, jnp.zeros((shots, stabs, width), jnp.float32), (jnp.moveaxis(decay, 1, 0), jnp.moveaxis(drive, 1, 0)))
    hidden = jnp.moveaxis(hidden, 0, 1)
    after_rec = after_attn + project(hidden.astype(jnp.bfloat16), w_rec_out)
    ffn_in = norm_rows(after_rec, gain_mlp)
    inner = (jax.nn.silu(project(ffn_in, w_gate)) * project(ffn_in, w_up)).astype(jnp.bfloat16)
    return (after_rec + project(inner, w_down)).astype(jnp.bfloat16)
```

```python
import functools

import jax
import jax.numpy as jnp
from jax import lax
from jax.experimental import pallas as pl
from jax.experimental.pallas import tpu as pltpu
from jax.sharding import PartitionSpec as P

HD = 32
LANES = 128
GROUP = 4
MESH = pl.DeviceIdType.MESH
F32 = jnp.float32
BF16 = jnp.bfloat16


def dot(left, right):
    return jnp.dot(left, right, preferred_element_type=F32)


def dot_t(left, right):
    return lax.dot_general(left, right, (((1,), (1,)), ((), ())), preferred_element_type=F32)


def norm_rows(values, gain):
    scale = lax.rsqrt(jnp.mean(values * values, axis=-1, keepdims=True) + 1e-05)
    return values * scale * gain


def pack(rows):
    return jnp.concatenate([rows[:, :LANES], rows[:, LANES:]], axis=0).astype(BF16)


def unpack(message):
    wide = message.astype(F32)
    half = wide.shape[0] // 2
    return jnp.concatenate([wide[:half], wide[half:]], axis=1)


def hop(slot):
    return (slot + 1) // 2 if slot % 2 else -(slot // 2)


def kernel(
    parts,
    blocks,
    states_ref,
    bits_ref,
    coords_ref,
    table_ref,
    flip_ref,
    gain_attn_ref,
    wq_ref,
    wk_ref,
    wv_ref,
    wo_ref,
    gain_rec_ref,
    wd_ref,
    bias_ref,
    wi_ref,
    wr_ref,
    gain_mlp_ref,
    wg_ref,
    wu_ref,
    wdown_ref,
    out_ref,
    small_ref,
    start_ref,
    send1,
    recv1,
    q_ref,
    k_ref,
    v_ref,
    send2,
    recv2,
    after_ref,
    decay_ref,
    drive_ref,
    send3,
    recv3,
    inc_ref,
    send1_sem,
    recv1_sem,
    send2_sem,
    recv2_sem,
    send3_sem,
    recv3_sem,
):
    shots, rounds, stabs, width = states_ref.shape
    rows = start_ref.shape[1]
    coord_rows = table_ref.shape[0]
    heads = width // HD
    gsize = GROUP * rows
    groups = parts // GROUP
    keys = parts * rows
    me = lax.axis_index("stab")
    block = lax.axis_index("round")

    def peer(offset):
        return lax.rem(me + (offset + parts), parts)

    barrier = pltpu.get_barrier_semaphore()
    for offset in range(1, parts):
        pl.semaphore_signal(barrier, inc=1, device_id={"stab": peer(offset)}, device_id_type=MESH)
    for offset in range(1, blocks):
        pl.semaphore_signal(
            barrier, inc=1, device_id={"round": lax.rem(block + offset, blocks)}, device_id_type=MESH
        )

    small_ref[...] = jnp.zeros_like(small_ref)
    small_ref[0:rounds, 0:stabs] = coords_ref[...].astype(F32)
    for shot in range(shots):
        first = rounds * (1 + shot)
        small_ref[first : first + rounds, 0:stabs] = bits_ref[shot].astype(F32)
    turned = jnp.transpose(small_ref[...])
    small_ref[...] = turned
    small_ref[stabs : stabs + 1, :] = small_ref[stabs - 1 : stabs, :]
    flip = flip_ref[...].astype(F32)
    gain_attn = gain_attn_ref[...].astype(F32)
    spot = lax.broadcasted_iota(jnp.int32, (rows, coord_rows), 1).astype(F32)
    for pair in range(rounds // 2):
        picks = []
        for t in (2 * pair, 2 * pair + 1):
            picks.append(jnp.where(small_ref[0:rows, t : t + 1] == spot, 1.0, 0.0))
        base = dot(jnp.concatenate(picks, axis=0).astype(BF16), table_ref[...])
        for half in range(2):
            t = 2 * pair + half
            for shot in range(shots):
                item = shot * rounds + t
                lane = rounds * (1 + shot) + t
                own = states_ref[shot, t].astype(F32)
                start_ref[item, 0:stabs, :] = own
                start_ref[item, stabs : stabs + 1, :] = own[stabs - 1 : stabs, :]
                sign = 2.0 * small_ref[0:rows, lane : lane + 1] - 1.0
                start = start_ref[item] + base[half * rows : (half + 1) * rows] + sign * flip
                start_ref[item] = start
                send1[item] = pack(norm_rows(start, gain_attn))

    pl.semaphore_wait(barrier, parts - 1 + blocks - 1)

    def copy1(slot):
        offset = hop(slot)
        back = slot if slot in (0, parts - 1) else (slot + 1 if slot % 2 else slot - 1)
        return pltpu.make_async_remote_copy(
            src_ref=send1.at[peer(offset)],
            dst_ref=recv1.at[back],
            send_sem=send1_sem.at[slot],
            recv_sem=recv1_sem.at[back],
            device_id={"stab": peer(offset)},
            device_id_type=MESH,
        )

    for slot in range(parts - 1, 0, -1):
        copy1(slot).start()
    recv1[0] = send1[me]

    real = lax.rem(lax.broadcasted_iota(jnp.int32, (gsize, 1), 0), rows) < stabs
    for group in range(groups):
        pieces = []
        for slot in range(group * GROUP, (group + 1) * GROUP):
            if slot:
                pltpu.make_async_remote_copy(
                    src_ref=send1.at[0],
                    dst_ref=recv1.at[slot],
                    send_sem=send1_sem.at[slot],
                    recv_sem=recv1_sem.at[slot],
                    device_id={"stab": peer(1)},
                    device_id_type=MESH,
                ).wait_recv()
            pieces.append(unpack(recv1[slot]))
        normed = jnp.concatenate(pieces, axis=0).astype(BF16)
        where = slice(group * gsize, (group + 1) * gsize)
        q_ref[where, :] = dot(normed, wq_ref[...]).astype(BF16)
        k_ref[where, :] = dot(normed, wk_ref[...]).astype(BF16)
        value = dot(normed, wv_ref[...])
        head_of = lax.broadcasted_iota(jnp.int32, (gsize, width), 1) // HD
        for head in range(heads):
            mine = jnp.where(head_of == head, value, 1.0)
            v_ref[head, where, :] = jnp.where(real, mine, 0.0).astype(BF16)

    head_of = lax.broadcasted_iota(jnp.int32, (gsize, width), 1) // HD

    def copy2(slot, target):
        return pltpu.make_async_remote_copy(
            src_ref=send2.at[slot],
            dst_ref=recv2.at[me],
            send_sem=send2_sem.at[slot],
            recv_sem=recv2_sem.at[me],
            device_id={"stab": target},
            device_id_type=MESH,
        )

    def attend(step, _):
        group = groups - 1 - step
        first = pl.multiple_of(group * gsize, gsize)
        query = q_ref[pl.ds(first, gsize), :].astype(F32)
        above = jnp.zeros((gsize, width), F32)
        below = jnp.ones((gsize, width), F32)
        for head in range(heads):
            mine = jnp.where(head_of == head, query, 0.0).astype(BF16)
            scores = dot_t(mine, k_ref[...]) * HD ** (-0.5)
            peak = jnp.max(scores, axis=-1, keepdims=True)
            weights = jnp.exp(scores - peak).astype(BF16)
            both = dot(weights, v_ref[head])
            above = jnp.where(head_of == head, both, above)
            below = jnp.where(head_of == head, pltpu.roll(both, LANES, 1), below)
        mixed = above / below
        for index in range(GROUP):
            slot = group * GROUP + index
            send2[slot] = pack(mixed[index * rows : (index + 1) * rows])
        for index in range(GROUP - 1, -1, -1):
            slot = group * GROUP + index
            half = lax.div(slot + 1, 2)
            offset = jnp.where(lax.rem(slot, 2) == 1, half, -half)

            @pl.when(slot > 0)
            def _():
                copy2(slot, peer(offset)).start()

        return 0

    lax.fori_loop(0, groups, attend, 0)
    recv2[me] = send2[0]

    gain_rec = gain_rec_ref[...].astype(F32)
    for group in range(groups - 1, -1, -1):
        pieces, starts = [], []
        for slot in range(group * GROUP, (group + 1) * GROUP):
            item = peer(hop(slot))
            if slot:
                pltpu.make_async_remote_copy(
                    src_ref=send2.at[0],
                    dst_ref=recv2.at[item],
                    send_sem=send2_sem.at[slot],
                    recv_sem=recv2_sem.at[item],
                    device_id={"stab": peer(1)},
                    device_id_type=MESH,
                ).wait_recv()
            pieces.append(unpack(recv2[item]))
            starts.append(start_ref[item])
        mixed = jnp.concatenate(pieces, axis=0).astype(BF16)
        after = jnp.concatenate(starts, axis=0) + dot(mixed, wo_ref[...])
        rec_in = norm_rows(after, gain_rec).astype(BF16)
        decay = jax.nn.sigmoid(dot(rec_in, wd_ref[...]) + bias_ref[...])
        drive = (1.0 - decay) * dot(rec_in, wi_ref[...])
        for index in range(GROUP):
            item = peer(hop(group * GROUP + index))
            part = slice(index * rows, (index + 1) * rows)
            after_ref[item] = after[part]
            decay_ref[item] = decay[part]
            drive_ref[item] = drive[part]

    for shot in range(shots):
        state = drive_ref[shot * rounds]
        product = decay_ref[shot * rounds]
        for t in range(1, rounds):
            item = shot * rounds + t
            decay = decay_ref[item]
            state = decay * state + drive_ref[item]
            product = product * decay
            drive_ref[item] = state
            decay_ref[item] = product
        send3[shot, 0] = pack(product)
        send3[shot, 1] = pack(state)

    def copy3(offset):
        return pltpu.make_async_remote_copy(
            src_ref=send3,
            dst_ref=recv3.at[offset],
            send_sem=send3_sem.at[offset],
            recv_sem=recv3_sem.at[offset],
            device_id={"round": lax.rem(block + offset, blocks)},
            device_id_type=MESH,
        )

    for offset in range(1, blocks):

        @pl.when(block + offset < blocks)
        def _():
            copy3(offset).start()

    inc_ref[...] = jnp.zeros_like(inc_ref)
    for offset in range(blocks - 1, 0, -1):

        @pl.when(block >= offset)
        def _():
            copy3(offset).wait_recv()
            for shot in range(shots):
                product = unpack(recv3[offset, shot, 0])
                inc_ref[shot] = product * inc_ref[shot] + unpack(recv3[offset, shot, 1])

    gain_mlp = gain_mlp_ref[...].astype(F32)

    def finish(group, _):
        hiddens, afters = [], []
        for index in range(GROUP):
            item = group * GROUP + index
            shot = lax.div(item, rounds)
            hiddens.append(drive_ref[item] + decay_ref[item] * inc_ref[shot])
            afters.append(after_ref[item])
        hidden = jnp.concatenate(hiddens, axis=0).astype(BF16)
        after = jnp.concatenate(afters, axis=0) + dot(hidden, wr_ref[...])
        ffn_in = norm_rows(after, gain_mlp).astype(BF16)
        inner = (jax.nn.silu(dot(ffn_in, wg_ref[...])) * dot(ffn_in, wu_ref[...])).astype(BF16)
        states = after + dot(inner, wdown_ref[...])
        for index in range(GROUP):
            item = group * GROUP + index
            out_ref[lax.div(item, rounds), lax.rem(item, rounds)] = states[
                index * rows : index * rows + stabs
            ].astype(BF16)
        return 0

    lax.fori_loop(0, groups, finish, 0)

    for slot in range(1, parts):
        copy1(slot).wait_send()
        copy2(slot, peer(1)).wait_send()
    for offset in range(1, blocks):

        @pl.when(block + offset < blocks)
        def _():
            copy3(offset).wait_send()


def body(parts, blocks, *args):
    states_in, coord_table = args[0], args[3]
    shots, rounds, stabs, width = states_in.shape
    assert shots * rounds == parts
    rows = -(-stabs // 8) * 8
    flat = [arg.reshape(1, -1) if arg.ndim == 1 else arg for arg in args]
    message = (2 * rows, LANES)
    vmem = pl.BlockSpec(memory_space=pltpu.VMEM)
    dma = pltpu.SemaphoreType.DMA
    return pl.pallas_call(
        functools.partial(kernel, parts, blocks),
        out_shape=jax.ShapeDtypeStruct(states_in.shape, BF16),
        in_specs=[vmem] * len(flat),
        out_specs=vmem,
        scratch_shapes=[
            pltpu.VMEM((LANES, LANES), F32),
            pltpu.VMEM((parts, rows, width), F32),
            pltpu.VMEM((parts,) + message, BF16),
            pltpu.VMEM((parts,) + message, BF16),
            pltpu.VMEM((parts * rows, width), BF16),
            pltpu.VMEM((parts * rows, width), BF16),
            pltpu.VMEM((width // HD, parts * rows, width), BF16),
            pltpu.VMEM((parts,) + message, BF16),
            pltpu.VMEM((parts,) + message, BF16),
            pltpu.VMEM((parts, rows, width), F32),
            pltpu.VMEM((parts, rows, width), F32),
            pltpu.VMEM((parts, rows, width), F32),
            pltpu.VMEM((shots, 2) + message, BF16),
            pltpu.VMEM((blocks, shots, 2) + message, BF16),
            pltpu.VMEM((shots, rows, width), F32),
            dma((parts,)),
            dma((parts,)),
            dma((parts,)),
            dma((parts,)),
            dma((blocks,)),
            dma((blocks,)),
        ],
        compiler_params=pltpu.CompilerParams(
            collective_id=0, has_side_effects=True, vmem_limit_bytes=48 * 1024 * 1024
        ),
    )(*flat)


def solution(mesh):
    placed = (P("shot", "round", "stab", None), P("shot", "round", "stab"), P("round", "stab")) + (P(),) * 16
    return jax.shard_map(
        functools.partial(body, mesh.shape["stab"], mesh.shape["round"]),
        mesh=mesh,
        in_specs=placed,
        out_specs=P("shot", "round", "stab", None),
        check_vma=False,
    )
```

```python
import functools

import jax
import jax.numpy as jnp
from jax import lax
from jax.experimental import pallas as pl
from jax.experimental.pallas import tpu as pltpu
from jax.sharding import PartitionSpec as P

HD = 32
LANES = 128
GROUP = 4
INPUTS = 19
MESH = pl.DeviceIdType.MESH
F32 = jnp.float32
BF16 = jnp.bfloat16


def dot(left, right):
    return jnp.dot(left, right, preferred_element_type=F32)


def dot_t(left, right):
    return lax.dot_general(left, right, (((1,), (1,)), ((), ())), preferred_element_type=F32)


def norm_rows(values, gain):
    scale = lax.rsqrt(jnp.mean(values * values, axis=-1, keepdims=True) + 1e-05)
    return values * scale * gain


def row(ref):
    return ref[...].astype(F32).reshape(1, -1)


def pack(rows):
    return jnp.concatenate([rows[:, :LANES], rows[:, LANES:]], axis=0).astype(BF16)


def unpack(message):
    wide = message.astype(F32)
    half = wide.shape[0] // 2
    return jnp.concatenate([wide[:half], wide[half:]], axis=1)


def hop(slot):
    return (slot + 1) // 2 if slot % 2 else -(slot // 2)


def kernel(parts, blocks, *refs):
    sources, refs = refs[:INPUTS], refs[INPUTS:]
    out_ref, refs = refs[0], refs[1:]
    operands, refs = refs[:INPUTS], refs[INPUTS:]
    run(parts, blocks, sources, out_ref, operands, *refs)


def run(
    parts,
    blocks,
    sources,
    out_ref,
    operands,
    wide_ref,
    small_ref,
    start_ref,
    send1,
    recv1,
    q_ref,
    k_ref,
    v_ref,
    send2,
    recv2,
    after_ref,
    decay_ref,
    drive_ref,
    send3,
    recv3,
    inc_ref,
    send1_sem,
    recv1_sem,
    send2_sem,
    recv2_sem,
    send3_sem,
    recv3_sem,
    load_sem,
):
    (states_ref, bits_ref, coords_ref, table_ref, flip_ref, gain_attn_ref, wq_ref, wk_ref, wv_ref, wo_ref) = operands[:10]
    (gain_rec_ref, wd_ref, bias_ref, wi_ref, wr_ref, gain_mlp_ref, wg_ref, wu_ref, wdown_ref) = operands[10:]
    shots, rounds, stabs = bits_ref.shape
    width = states_ref.shape[1]
    rows = start_ref.shape[1]
    coord_rows = table_ref.shape[0]
    heads = width // HD
    gsize = GROUP * rows
    groups = parts // GROUP
    keys = parts * rows
    me = lax.axis_index("stab")
    block = lax.axis_index("round")

    def peer(offset):
        return lax.rem(me + (offset + parts), parts)

    def load(index):
        return pltpu.make_async_copy(sources[index], operands[index], load_sem.at[index])

    barrier = pltpu.get_barrier_semaphore()
    for offset in range(1, parts):
        pl.semaphore_signal(barrier, inc=1, device_id={"stab": peer(offset)}, device_id_type=MESH)
    for offset in range(1, blocks):
        pl.semaphore_signal(
            barrier, inc=1, device_id={"round": lax.rem(block + offset, blocks)}, device_id_type=MESH
        )

    for index in range(INPUTS):
        load(index).start()

    for index in range(6):
        load(index).wait()
    for half in range(2):
        wide_ref[half] = states_ref[:, half * LANES : (half + 1) * LANES].astype(F32)
    small_ref[...] = jnp.zeros_like(small_ref)
    small_ref[0:rounds, 0:stabs] = coords_ref[...].astype(F32)
    for shot in range(shots):
        first = rounds * (1 + shot)
        small_ref[first : first + rounds, 0:stabs] = bits_ref[shot].astype(F32)
    turned = jnp.transpose(small_ref[...])
    small_ref[...] = turned
    small_ref[stabs : stabs + 1, :] = small_ref[stabs - 1 : stabs, :]
    flip = row(flip_ref)
    gain_attn = row(gain_attn_ref)
    spot = lax.broadcasted_iota(jnp.int32, (rows, coord_rows), 1).astype(F32)
    for pair in range(rounds // 2):
        picks = []
        for t in (2 * pair, 2 * pair + 1):
            picks.append(jnp.where(small_ref[0:rows, t : t + 1] == spot, 1.0, 0.0))
        base = dot(jnp.concatenate(picks, axis=0).astype(BF16), table_ref[...])
        for half in range(2):
            t = 2 * pair + half
            for shot in range(shots):
                item = shot * rounds + t
                lane = rounds * (1 + shot) + t
                where = pl.ds(shot * stabs * rounds + t, stabs, stride=rounds)
                own = jnp.concatenate([wide_ref[0, where, :], wide_ref[1, where, :]], axis=1)
                start_ref[item, 0:stabs, :] = own
                start_ref[item, stabs : stabs + 1, :] = own[stabs - 1 : stabs, :]
                sign = 2.0 * small_ref[0:rows, lane : lane + 1] - 1.0
                start = start_ref[item] + base[half * rows : (half + 1) * rows] + sign * flip
                start_ref[item] = start
                send1[item] = pack(norm_rows(start, gain_attn))

    pl.semaphore_wait(barrier, parts - 1 + blocks - 1)

    def copy1(slot):
        offset = hop(slot)
        back = slot if slot in (0, parts - 1) else (slot + 1 if slot % 2 else slot - 1)
        return pltpu.make_async_remote_copy(
            src_ref=send1.at[peer(offset)],
            dst_ref=recv1.at[back],
            send_sem=send1_sem.at[slot],
            recv_sem=recv1_sem.at[back],
            device_id={"stab": peer(offset)},
            device_id_type=MESH,
        )

    for slot in range(parts - 1, 0, -1):
        copy1(slot).start()
    recv1[0] = send1[me]

    for index in range(6, INPUTS):
        load(index).wait()
    real = lax.rem(lax.broadcasted_iota(jnp.int32, (gsize, 1), 0), rows) < stabs
    for group in range(groups):
        pieces = []
        for slot in range(group * GROUP, (group + 1) * GROUP):
            if slot:
                pltpu.make_async_remote_copy(
                    src_ref=send1.at[0],
                    dst_ref=recv1.at[slot],
                    send_sem=send1_sem.at[slot],
                    recv_sem=recv1_sem.at[slot],
                    device_id={"stab": peer(1)},
                    device_id_type=MESH,
                ).wait_recv()
            pieces.append(unpack(recv1[slot]))
        normed = jnp.concatenate(pieces, axis=0).astype(BF16)
        where = slice(group * gsize, (group + 1) * gsize)
        q_ref[where, :] = dot(normed, wq_ref[...]).astype(BF16)
        k_ref[where, :] = dot(normed, wk_ref[...]).astype(BF16)
        value = dot(normed, wv_ref[...])
        head_of = lax.broadcasted_iota(jnp.int32, (gsize, width), 1) // HD
        for head in range(heads):
            mine = jnp.where(head_of == head, value, 1.0)
            v_ref[head, where, :] = jnp.where(real, mine, 0.0).astype(BF16)

    head_of = lax.broadcasted_iota(jnp.int32, (gsize, width), 1) // HD

    def copy2(slot, target):
        return pltpu.make_async_remote_copy(
            src_ref=send2.at[slot],
            dst_ref=recv2.at[me],
            send_sem=send2_sem.at[slot],
            recv_sem=recv2_sem.at[me],
            device_id={"stab": target},
            device_id_type=MESH,
        )

    def attend(step, _):
        group = groups - 1 - step
        first = pl.multiple_of(group * gsize, gsize)
        query = q_ref[pl.ds(first, gsize), :].astype(F32)
        above = jnp.zeros((gsize, width), F32)
        below = jnp.ones((gsize, width), F32)
        for head in range(heads):
            mine = jnp.where(head_of == head, query, 0.0).astype(BF16)
            scores = dot_t(mine, k_ref[...]) * HD ** (-0.5)
            peak = jnp.max(scores, axis=-1, keepdims=True)
            weights = jnp.exp(scores - peak).astype(BF16)
            both = dot(weights, v_ref[head])
            above = jnp.where(head_of == head, both, above)
            below = jnp.where(head_of == head, pltpu.roll(both, LANES, 1), below)
        mixed = above / below
        for index in range(GROUP):
            slot = group * GROUP + index
            send2[slot] = pack(mixed[index * rows : (index + 1) * rows])
        for index in range(GROUP - 1, -1, -1):
            slot = group * GROUP + index
            half = lax.div(slot + 1, 2)
            offset = jnp.where(lax.rem(slot, 2) == 1, half, -half)

            @pl.when(slot > 0)
            def _():
                copy2(slot, peer(offset)).start()

        return 0

    lax.fori_loop(0, groups, attend, 0)
    recv2[me] = send2[0]

    gain_rec = row(gain_rec_ref)
    for group in range(groups - 1, -1, -1):
        pieces, starts = [], []
        for slot in range(group * GROUP, (group + 1) * GROUP):
            item = peer(hop(slot))
            if slot:
                pltpu.make_async_remote_copy(
                    src_ref=send2.at[0],
                    dst_ref=recv2.at[item],
                    send_sem=send2_sem.at[slot],
                    recv_sem=recv2_sem.at[item],
                    device_id={"stab": peer(1)},
                    device_id_type=MESH,
                ).wait_recv()
            pieces.append(unpack(recv2[item]))
            starts.append(start_ref[item])
        mixed = jnp.concatenate(pieces, axis=0).astype(BF16)
        after = jnp.concatenate(starts, axis=0) + dot(mixed, wo_ref[...])
        rec_in = norm_rows(after, gain_rec).astype(BF16)
        decay = jax.nn.sigmoid(dot(rec_in, wd_ref[...]) + row(bias_ref))
        drive = (1.0 - decay) * dot(rec_in, wi_ref[...])
        for index in range(GROUP):
            item = peer(hop(group * GROUP + index))
            part = slice(index * rows, (index + 1) * rows)
            after_ref[item] = after[part]
            decay_ref[item] = decay[part]
            drive_ref[item] = drive[part]

    for shot in range(shots):
        state = drive_ref[shot * rounds]
        product = decay_ref[shot * rounds]
        for t in range(1, rounds):
            item = shot * rounds + t
            decay = decay_ref[item]
            state = decay * state + drive_ref[item]
            product = product * decay
            drive_ref[item] = state
            decay_ref[item] = product
        send3[shot, 0] = pack(product)
        send3[shot, 1] = pack(state)

    def copy3(offset):
        return pltpu.make_async_remote_copy(
            src_ref=send3,
            dst_ref=recv3.at[offset],
            send_sem=send3_sem.at[offset],
            recv_sem=recv3_sem.at[offset],
            device_id={"round": lax.rem(block + offset, blocks)},
            device_id_type=MESH,
        )

    for offset in range(1, blocks):

        @pl.when(block + offset < blocks)
        def _():
            copy3(offset).start()

    inc_ref[...] = jnp.zeros_like(inc_ref)
    for offset in range(blocks - 1, 0, -1):

        @pl.when(block >= offset)
        def _():
            copy3(offset).wait_recv()
            for shot in range(shots):
                product = unpack(recv3[offset, shot, 0])
                inc_ref[shot] = product * inc_ref[shot] + unpack(recv3[offset, shot, 1])

    gain_mlp = row(gain_mlp_ref)

    def finish(group, _):
        hiddens, afters = [], []
        for index in range(GROUP):
            item = group * GROUP + index
            shot = lax.div(item, rounds)
            hiddens.append(drive_ref[item] + decay_ref[item] * inc_ref[shot])
            afters.append(after_ref[item])
        hidden = jnp.concatenate(hiddens, axis=0).astype(BF16)
        after = jnp.concatenate(afters, axis=0) + dot(hidden, wr_ref[...])
        ffn_in = norm_rows(after, gain_mlp).astype(BF16)
        inner = (jax.nn.silu(dot(ffn_in, wg_ref[...])) * dot(ffn_in, wu_ref[...])).astype(BF16)
        states = after + dot(inner, wdown_ref[...])
        for index in range(GROUP):
            item = group * GROUP + index
            first = lax.div(item, rounds) * (stabs * rounds) + lax.rem(item, rounds)
            for half in range(2):
                wide_ref[half, pl.ds(first, stabs, stride=rounds), :] = states[
                    index * rows : index * rows + stabs, half * LANES : (half + 1) * LANES
                ]
        return 0

    lax.fori_loop(0, groups, finish, 0)
    for half in range(2):
        out_ref[:, half * LANES : (half + 1) * LANES] = wide_ref[half].astype(BF16)

    for slot in range(1, parts):
        copy1(slot).wait_send()
        copy2(slot, peer(1)).wait_send()
    for offset in range(1, blocks):

        @pl.when(block + offset < blocks)
        def _():
            copy3(offset).wait_send()


def body(parts, blocks, *args):
    states_in = args[0]
    shots, rounds, stabs, width = states_in.shape
    assert shots * rounds == parts
    assert len(args) == INPUTS
    rows = -(-stabs // 8) * 8
    flat = (jnp.transpose(states_in, (0, 2, 1, 3)).reshape(-1, width),) + args[1:]
    message = (2 * rows, LANES)
    vmem = pl.BlockSpec(memory_space=pltpu.VMEM)
    dma = pltpu.SemaphoreType.DMA
    result = pl.pallas_call(
        functools.partial(kernel, parts, blocks),
        out_shape=jax.ShapeDtypeStruct(flat[0].shape, BF16),
        in_specs=[pl.BlockSpec(memory_space=pltpu.HBM)] * len(flat),
        out_specs=vmem,
        scratch_shapes=[pltpu.VMEM(arg.shape, arg.dtype) for arg in flat]
        + [
            pltpu.VMEM((2, flat[0].shape[0], LANES), F32),
            pltpu.VMEM((LANES, LANES), F32),
            pltpu.VMEM((parts, rows, width), F32),
            pltpu.VMEM((parts,) + message, BF16),
            pltpu.VMEM((parts,) + message, BF16),
            pltpu.VMEM((parts * rows, width), BF16),
            pltpu.VMEM((parts * rows, width), BF16),
            pltpu.VMEM((width // HD, parts * rows, width), BF16),
            pltpu.VMEM((parts,) + message, BF16),
            pltpu.VMEM((parts,) + message, BF16),
            pltpu.VMEM((parts, rows, width), F32),
            pltpu.VMEM((parts, rows, width), F32),
            pltpu.VMEM((parts, rows, width), F32),
            pltpu.VMEM((shots, 2) + message, BF16),
            pltpu.VMEM((blocks, shots, 2) + message, BF16),
            pltpu.VMEM((shots, rows, width), F32),
            dma((parts,)),
            dma((parts,)),
            dma((parts,)),
            dma((parts,)),
            dma((blocks,)),
            dma((blocks,)),
            dma((INPUTS,)),
        ],
        compiler_params=pltpu.CompilerParams(
            collective_id=0, has_side_effects=True, vmem_limit_bytes=58 * 1024 * 1024
        ),
    )(*flat)
    return jnp.transpose(result.reshape(shots, stabs, rounds, width), (0, 2, 1, 3))


def solution(mesh):
    placed = (P("shot", "round", "stab", None), P("shot", "round", "stab"), P("round", "stab")) + (P(),) * 16
    return jax.shard_map(
        functools.partial(body, mesh.shape["stab"], mesh.shape["round"]),
        mesh=mesh,
        in_specs=placed,
        out_specs=P("shot", "round", "stab", None),
        check_vma=False,
    )
```

```python
import functools
import math

import jax
import jax.numpy as jnp
from jax import lax
from jax.experimental import pallas as pl
from jax.experimental.pallas import tpu as pltpu
from jax.sharding import PartitionSpec as P

HD = 32
LANES = 128
GROUP = 4
INPUTS = 19
QUERIES = 256
MESH = pl.DeviceIdType.MESH
F32 = jnp.float32
BF16 = jnp.bfloat16


def dot(left, right):
    return jnp.dot(left, right, preferred_element_type=F32)


def dot_t(left, right):
    return lax.dot_general(left, right, (((1,), (1,)), ((), ())), preferred_element_type=F32)


def norm_rows(values, gain):
    scale = lax.rsqrt(jnp.mean(values * values, axis=-1, keepdims=True) + 1e-05)
    return values * scale * gain


def row(ref):
    return ref[...].astype(F32).reshape(1, -1)


def pack(rows):
    return jnp.concatenate([rows[:, :LANES], rows[:, LANES:]], axis=0).astype(BF16)


def unpack(message):
    wide = message.astype(F32)
    half = wide.shape[0] // 2
    return jnp.concatenate([wide[:half], wide[half:]], axis=1)


def hop(slot):
    return (slot + 1) // 2 if slot % 2 else -(slot // 2)


def kernel(parts, blocks, *refs):
    sources, refs = refs[:INPUTS], refs[INPUTS:]
    out_ref, refs = refs[0], refs[1:]
    operands, refs = refs[:INPUTS], refs[INPUTS:]
    run(parts, blocks, sources, out_ref, operands, *refs)


def run(
    parts,
    blocks,
    sources,
    out_ref,
    operands,
    wide_ref,
    small_ref,
    start_ref,
    send1,
    recv1,
    q_ref,
    k_ref,
    v_ref,
    n_ref,
    turned_ref,
    across_ref,
    mixed_ref,
    send2,
    recv2,
    after_ref,
    decay_ref,
    drive_ref,
    send3,
    recv3,
    send4,
    recv4,
    inc_ref,
    send1_sem,
    recv1_sem,
    send2_sem,
    recv2_sem,
    send3_sem,
    recv3_sem,
    send4_sem,
    recv4_sem,
    load_sem,
):
    (states_ref, bits_ref, coords_ref, table_ref, flip_ref, gain_attn_ref, wq_ref, wk_ref, wv_ref, wo_ref) = operands[:10]
    (gain_rec_ref, wd_ref, bias_ref, wi_ref, wr_ref, gain_mlp_ref, wg_ref, wu_ref, wdown_ref) = operands[10:]
    shots, rounds, stabs = bits_ref.shape
    width = states_ref.shape[1]
    rows = start_ref.shape[1]
    coord_rows = table_ref.shape[0]
    heads = width // HD
    gsize = GROUP * rows
    groups = parts // GROUP
    keys = parts * rows
    me = lax.axis_index("stab")
    block = lax.axis_index("round")

    def peer(offset):
        return lax.rem(me + (offset + parts), parts)

    def load(index):
        return pltpu.make_async_copy(sources[index], operands[index], load_sem.at[index])

    barrier = pltpu.get_barrier_semaphore()
    for offset in range(1, parts):
        pl.semaphore_signal(barrier, inc=1, device_id={"stab": peer(offset)}, device_id_type=MESH)
    for offset in range(1, blocks):
        pl.semaphore_signal(
            barrier, inc=1, device_id={"round": lax.rem(block + offset, blocks)}, device_id_type=MESH
        )

    for index in range(INPUTS):
        load(index).start()

    for index in range(6):
        load(index).wait()
    for half in range(2):
        wide_ref[half] = states_ref[:, half * LANES : (half + 1) * LANES].astype(F32)
    small_ref[...] = jnp.zeros_like(small_ref)
    small_ref[0:rounds, 0:stabs] = coords_ref[...].astype(F32)
    for shot in range(shots):
        first = rounds * (1 + shot)
        small_ref[first : first + rounds, 0:stabs] = bits_ref[shot].astype(F32)
    turned = jnp.transpose(small_ref[...])
    small_ref[...] = turned
    small_ref[stabs : stabs + 1, :] = small_ref[stabs - 1 : stabs, :]
    flip = row(flip_ref)
    gain_attn = row(gain_attn_ref)
    spot = lax.broadcasted_iota(jnp.int32, (rows, coord_rows), 1).astype(F32)
    for pair in range(rounds // 2):
        picks = []
        for t in (2 * pair, 2 * pair + 1):
            picks.append(jnp.where(small_ref[0:rows, t : t + 1] == spot, 1.0, 0.0))
        base = dot(jnp.concatenate(picks, axis=0).astype(BF16), table_ref[...])
        for half in range(2):
            t = 2 * pair + half
            for shot in range(shots):
                item = shot * rounds + t
                lane = rounds * (1 + shot) + t
                where = pl.ds(shot * stabs * rounds + t, stabs, stride=rounds)
                own = jnp.concatenate([wide_ref[0, where, :], wide_ref[1, where, :]], axis=1)
                start_ref[item, 0:stabs, :] = own
                start_ref[item, stabs : stabs + 1, :] = own[stabs - 1 : stabs, :]
                sign = 2.0 * small_ref[0:rows, lane : lane + 1] - 1.0
                start = start_ref[item] + base[half * rows : (half + 1) * rows] + sign * flip
                start_ref[item] = start
                send1[item] = pack(norm_rows(start, gain_attn))

    pl.semaphore_wait(barrier, parts - 1 + blocks - 1)

    def copy1(slot):
        offset = hop(slot)
        back = slot if slot in (0, parts - 1) else (slot + 1 if slot % 2 else slot - 1)
        return pltpu.make_async_remote_copy(
            src_ref=send1.at[peer(offset)],
            dst_ref=recv1.at[back],
            send_sem=send1_sem.at[slot],
            recv_sem=recv1_sem.at[back],
            device_id={"stab": peer(offset)},
            device_id_type=MESH,
        )

    for slot in range(parts - 1, 0, -1):
        copy1(slot).start()
    recv1[0] = send1[me]

    for index in range(6, INPUTS):
        load(index).wait()
    turned_ref[...] = jnp.transpose(wv_ref[...].astype(F32)).astype(BF16)
    for group in range(groups):
        pieces = []
        for slot in range(group * GROUP, (group + 1) * GROUP):
            if slot:
                pltpu.make_async_remote_copy(
                    src_ref=send1.at[0],
                    dst_ref=recv1.at[slot],
                    send_sem=send1_sem.at[slot],
                    recv_sem=recv1_sem.at[slot],
                    device_id={"stab": peer(1)},
                    device_id_type=MESH,
                ).wait_recv()
            pieces.append(unpack(recv1[slot]))
        normed = jnp.concatenate(pieces, axis=0).astype(BF16)
        where = slice(group * gsize, (group + 1) * gsize)
        q_ref[where, :] = dot(normed, wq_ref[...]).astype(BF16)
        k_ref[where, :] = dot(normed, wk_ref[...]).astype(BF16)
        n_ref[where, :] = normed
    real = lax.rem(lax.broadcasted_iota(jnp.int32, (1, keys), 1), rows) < stabs
    values = jnp.where(real, dot_t(turned_ref[...], n_ref[...]), 0.0)
    ones = jnp.where(real, jnp.ones((v_ref.shape[1] - HD, keys), F32), 0.0).astype(BF16)
    for head in range(heads):
        v_ref[head, 0:HD, :] = values[head * HD : (head + 1) * HD].astype(BF16)
        v_ref[head, HD:, :] = ones

    def copy2(slot, target):
        return pltpu.make_async_remote_copy(
            src_ref=send2.at[slot],
            dst_ref=recv2.at[me],
            send_sem=send2_sem.at[slot],
            recv_sem=recv2_sem.at[me],
            device_id={"stab": target},
            device_id_type=MESH,
        )

    scale = HD ** (-0.5) * math.log2(math.e)
    done = parts
    for last in range(keys, 0, -QUERIES):
        first = max(last - QUERIES, 0)
        count = last - first
        query = q_ref[first:last, :].astype(F32)
        head_of = lax.broadcasted_iota(jnp.int32, (count, width), 1) // HD
        for head in range(heads):
            mine = jnp.where(head_of == head, query, 0.0).astype(BF16)
            scores = dot_t(k_ref[...], mine)
            peak = jnp.max(scores, axis=0, keepdims=True)
            weights = jnp.exp2((scores - peak) * scale).astype(BF16)
            both = dot(v_ref[head], weights)
            across_ref[head * HD : (head + 1) * HD, 0:count] = both[:HD] / both[HD : HD + 1]
        mixed_ref[first:last, :] = jnp.transpose(across_ref[:, 0:count])
        while done > 0 and (done - 1) * rows >= first:
            done -= 1
            send2[done] = pack(mixed_ref[done * rows : (done + 1) * rows, :])
            if done:
                copy2(done, peer(hop(done))).start()
    recv2[me] = send2[0]

    gain_rec = row(gain_rec_ref)
    for group in range(groups - 1, -1, -1):
        pieces, starts = [], []
        for slot in range(group * GROUP, (group + 1) * GROUP):
            item = peer(hop(slot))
            if slot:
                pltpu.make_async_remote_copy(
                    src_ref=send2.at[0],
                    dst_ref=recv2.at[item],
                    send_sem=send2_sem.at[slot],
                    recv_sem=recv2_sem.at[item],
                    device_id={"stab": peer(1)},
                    device_id_type=MESH,
                ).wait_recv()
            pieces.append(unpack(recv2[item]))
            starts.append(start_ref[item])
        mixed = jnp.concatenate(pieces, axis=0).astype(BF16)
        after = jnp.concatenate(starts, axis=0) + dot(mixed, wo_ref[...])
        rec_in = norm_rows(after, gain_rec).astype(BF16)
        decay = jax.nn.sigmoid(dot(rec_in, wd_ref[...]) + row(bias_ref))
        drive = (1.0 - decay) * dot(rec_in, wi_ref[...])
        for index in range(GROUP):
            item = peer(hop(group * GROUP + index))
            part = slice(index * rows, (index + 1) * rows)
            after_ref[item] = after[part]
            decay_ref[item] = decay[part]
            drive_ref[item] = drive[part]

    for shot in range(shots):
        state = drive_ref[shot * rounds]
        product = decay_ref[shot * rounds]
        for t in range(1, rounds):
            item = shot * rounds + t
            decay = decay_ref[item]
            state = decay * state + drive_ref[item]
            product = product * decay
            drive_ref[item] = state
            decay_ref[item] = product
        for half in range(2):
            part = slice(half * LANES, (half + 1) * LANES)
            send3[2 * shot + half] = jnp.concatenate([product[:, part], state[:, part]], axis=0).astype(BF16)

    chunks = 2 * shots
    step = blocks // chunks
    shift = lax.rem(lax.axis_index("shot"), step)
    my_chunk = lax.div(block, step)
    owner = lax.rem(block, step) == shift

    def copy3(chunk):
        return pltpu.make_async_remote_copy(
            src_ref=send3.at[chunk],
            dst_ref=recv3.at[block],
            send_sem=send3_sem.at[chunk],
            recv_sem=recv3_sem.at[block],
            device_id={"round": chunk * step + shift},
            device_id_type=MESH,
        )

    def copy4(target):
        return pltpu.make_async_remote_copy(
            src_ref=send4.at[target],
            dst_ref=recv4.at[my_chunk],
            send_sem=send4_sem.at[target],
            recv_sem=recv4_sem.at[my_chunk],
            device_id={"round": target},
            device_id_type=MESH,
        )

    for chunk in range(chunks):

        @pl.when(block != chunk * step + shift)
        def _():
            copy3(chunk).start()

        @pl.when(block == chunk * step + shift)
        def _():
            recv3[block] = send3[chunk]

    @pl.when(owner)
    def _():
        entering = jnp.zeros((rows, LANES), F32)
        below = jnp.zeros((send4.shape[1] - rows, LANES), F32)
        for source in range(blocks):
            send4[source] = jnp.concatenate([entering, below], axis=0).astype(BF16)

            @pl.when(block != source)
            def _():
                copy4(source).start()
                pltpu.make_async_remote_copy(
                    src_ref=send3.at[0],
                    dst_ref=recv3.at[source],
                    send_sem=send3_sem.at[0],
                    recv_sem=recv3_sem.at[source],
                    device_id={"round": source},
                    device_id_type=MESH,
                ).wait_recv()

            wide = recv3[source].astype(F32)
            entering = wide[:rows] * entering + wide[rows:]
        recv4[my_chunk] = send4[block]

    for chunk in range(chunks):

        @pl.when(block != chunk * step + shift)
        def _():
            pltpu.make_async_remote_copy(
                src_ref=send4.at[0],
                dst_ref=recv4.at[chunk],
                send_sem=send4_sem.at[0],
                recv_sem=recv4_sem.at[chunk],
                device_id={"round": chunk * step + shift},
                device_id_type=MESH,
            ).wait_recv()

        part = slice((chunk % 2) * LANES, (chunk % 2 + 1) * LANES)
        inc_ref[chunk // 2, :, part] = recv4[chunk].astype(F32)[:rows]

    gain_mlp = row(gain_mlp_ref)

    def finish(group, _):
        hiddens, afters = [], []
        for index in range(GROUP):
            item = group * GROUP + index
            shot = lax.div(item, rounds)
            hiddens.append(drive_ref[item] + decay_ref[item] * inc_ref[shot])
            afters.append(after_ref[item])
        hidden = jnp.concatenate(hiddens, axis=0).astype(BF16)
        after = jnp.concatenate(afters, axis=0) + dot(hidden, wr_ref[...])
        ffn_in = norm_rows(after, gain_mlp).astype(BF16)
        inner = (jax.nn.silu(dot(ffn_in, wg_ref[...])) * dot(ffn_in, wu_ref[...])).astype(BF16)
        states = after + dot(inner, wdown_ref[...])
        for index in range(GROUP):
            item = group * GROUP + index
            first = lax.div(item, rounds) * (stabs * rounds) + lax.rem(item, rounds)
            for half in range(2):
                wide_ref[half, pl.ds(first, stabs, stride=rounds), :] = states[
                    index * rows : index * rows + stabs, half * LANES : (half + 1) * LANES
                ]
        return 0

    lax.fori_loop(0, groups, finish, 0)
    for half in range(2):
        out_ref[:, half * LANES : (half + 1) * LANES] = wide_ref[half].astype(BF16)

    for slot in range(1, parts):
        copy1(slot).wait_send()
        copy2(slot, peer(1)).wait_send()
    for chunk in range(chunks):

        @pl.when(block != chunk * step + shift)
        def _():
            copy3(chunk).wait_send()

    for target in range(blocks):

        @pl.when(owner & (block != target))
        def _():
            copy4(target).wait_send()


def body(parts, blocks, *args):
    states_in = args[0]
    shots, rounds, stabs, width = states_in.shape
    assert shots * rounds == parts
    assert len(args) == INPUTS
    rows = -(-stabs // 8) * 8
    flat = (jnp.transpose(states_in, (0, 2, 1, 3)).reshape(-1, width),) + args[1:]
    message = (2 * rows, LANES)
    vmem = pl.BlockSpec(memory_space=pltpu.VMEM)
    dma = pltpu.SemaphoreType.DMA
    result = pl.pallas_call(
        functools.partial(kernel, parts, blocks),
        out_shape=pltpu.VMEM(flat[0].shape, BF16),
        in_specs=[pl.BlockSpec(memory_space=pltpu.HBM)] * len(flat),
        out_specs=vmem,
        scratch_shapes=[pltpu.VMEM(arg.shape, arg.dtype) for arg in flat]
        + [
            pltpu.VMEM((2, flat[0].shape[0], LANES), F32),
            pltpu.VMEM((LANES, LANES), F32),
            pltpu.VMEM((parts, rows, width), F32),
            pltpu.VMEM((parts,) + message, BF16),
            pltpu.VMEM((parts,) + message, BF16),
            pltpu.VMEM((parts * rows, width), BF16),
            pltpu.VMEM((parts * rows, width), BF16),
            pltpu.VMEM((width // HD, HD + 16, parts * rows), BF16),
            pltpu.VMEM((parts * rows, width), BF16),
            pltpu.VMEM((width, width), BF16),
            pltpu.VMEM((width, QUERIES), F32),
            pltpu.VMEM((parts * rows, width), F32),
            pltpu.VMEM((parts,) + message, BF16),
            pltpu.VMEM((parts,) + message, BF16),
            pltpu.VMEM((parts, rows, width), F32),
            pltpu.VMEM((parts, rows, width), F32),
            pltpu.VMEM((parts, rows, width), F32),
            pltpu.VMEM((2 * shots,) + message, BF16),
            pltpu.VMEM((blocks,) + message, BF16),
            pltpu.VMEM((blocks, -(-rows // 16) * 16, LANES), BF16),
            pltpu.VMEM((2 * shots, -(-rows // 16) * 16, LANES), BF16),
            pltpu.VMEM((shots, rows, width), F32),
            dma((parts,)),
            dma((parts,)),
            dma((parts,)),
            dma((parts,)),
            dma((2 * shots,)),
            dma((blocks,)),
            dma((blocks,)),
            dma((2 * shots,)),
            dma((INPUTS,)),
        ],
        compiler_params=pltpu.CompilerParams(
            collective_id=0, has_side_effects=True, vmem_limit_bytes=58 * 1024 * 1024
        ),
    )(*flat)
    return jnp.transpose(result.reshape(shots, stabs, rounds, width), (0, 2, 1, 3))


def solution(mesh):
    placed = (P("shot", "round", "stab", None), P("shot", "round", "stab"), P("round", "stab")) + (P(),) * 16
    return jax.shard_map(
        functools.partial(body, mesh.shape["stab"], mesh.shape["round"]),
        mesh=mesh,
        in_specs=placed,
        out_specs=P("shot", "round", "stab", None),
        check_vma=False,
    )
```

```python
import functools
import math

import jax
import jax.numpy as jnp
from jax import lax
from jax.experimental import pallas as pl
from jax.experimental.pallas import tpu as pltpu
from jax.sharding import PartitionSpec as P

HD = 32
LANES = 128
GROUP = 4
INPUTS = 19
FINISH = 8
BASE = 32
COUNTS = (128, 256, 256)
ARRIVALS = ((0, 1, 2, 3), (4, 5, 6, 7), (8, 9, 10, 11), (12, 13), (14, 15))
MESH = pl.DeviceIdType.MESH
F32 = jnp.float32
BF16 = jnp.bfloat16


def dot(left, right):
    return jnp.dot(left, right, preferred_element_type=F32)


def dot_t(left, right):
    return lax.dot_general(left, right, (((1,), (1,)), ((), ())), preferred_element_type=F32)


def norm_rows(values, gain):
    scale = lax.rsqrt(jnp.mean(values * values, axis=-1, keepdims=True) + 1e-05)
    return values * scale * gain


def row(ref):
    return ref[...].astype(F32).reshape(1, -1)


def pack(rows):
    return jnp.concatenate([rows[:, :LANES], rows[:, LANES:]], axis=0).astype(BF16)


def unpack(message):
    wide = message.astype(F32)
    half = wide.shape[0] // 2
    return jnp.concatenate([wide[:half], wide[half:]], axis=1)


def hop(slot):
    return (slot + 1) // 2 if slot % 2 else -(slot // 2)


def kernel(parts, blocks, *refs):
    sources, refs = refs[:INPUTS], refs[INPUTS:]
    out_ref, refs = refs[0], refs[1:]
    operands, refs = refs[:INPUTS], refs[INPUTS:]
    run(parts, blocks, sources, out_ref, operands, *refs)


def run(
    parts,
    blocks,
    sources,
    out_ref,
    operands,
    wide_ref,
    small_ref,
    loose_ref,
    start_ref,
    send1,
    recv1,
    q_ref,
    k_ref,
    v_ref,
    n_ref,
    turned_ref,
    across_ref,
    mixed_ref,
    send2,
    recv2,
    after_ref,
    decay_ref,
    drive_ref,
    send3,
    recv3,
    send4,
    recv4,
    inc_ref,
    send1_sem,
    recv1_sem,
    send2_sem,
    recv2_sem,
    send3_sem,
    recv3_sem,
    send4_sem,
    recv4_sem,
    load_sem,
):
    (states_ref, bits_ref, coords_ref, table_ref, flip_ref, gain_attn_ref, wq_ref, wk_ref, wv_ref, wo_ref) = operands[:10]
    (gain_rec_ref, wd_ref, bias_ref, wi_ref, wr_ref, gain_mlp_ref, wg_ref, wu_ref, wdown_ref) = operands[10:]
    shots, rounds, stabs = bits_ref.shape
    width = states_ref.shape[1]
    rows = start_ref.shape[1]
    coord_rows = table_ref.shape[0]
    heads = width // HD
    gsize = GROUP * rows
    groups = parts // GROUP
    keys = parts * rows
    me = lax.axis_index("stab")
    block = lax.axis_index("round")

    def peer(offset):
        return lax.rem(me + (offset + parts), parts)

    def load(index):
        return pltpu.make_async_copy(sources[index], operands[index], load_sem.at[index])

    barrier = pltpu.get_barrier_semaphore()
    for offset in range(1, parts):
        pl.semaphore_signal(barrier, inc=1, device_id={"stab": peer(offset)}, device_id_type=MESH)
    for offset in range(1, blocks):
        pl.semaphore_signal(
            barrier, inc=1, device_id={"round": lax.rem(block + offset, blocks)}, device_id_type=MESH
        )

    for index in range(INPUTS):
        load(index).start()

    small_ref[...] = jnp.zeros_like(small_ref)
    for index in range(3):
        load(index).wait()
    for half in range(2):
        wide_ref[half] = states_ref[:, half * LANES : (half + 1) * LANES].astype(F32)
    coords = coords_ref[...]
    small_ref[0:rounds, 0:stabs] = (coords // BASE).astype(F32)
    for shot in range(shots):
        first = rounds * (1 + shot)
        small_ref[first : first + rounds, 0:stabs] = (coords % BASE + BASE * bits_ref[shot]).astype(F32)
    for item in range(parts):
        shot, t = divmod(item, rounds)
        where = pl.ds(shot * stabs * rounds + t, stabs, stride=rounds)
        for half in range(2):
            lane = t if half == 0 else rounds * (1 + shot) + t
            loose_ref[item, half * rows : half * rows + stabs, :] = wide_ref[half, where, :]
            loose_ref[item, half * rows + stabs : (half + 1) * rows, :] = small_ref[lane : lane + 1, :]
        send1[item] = loose_ref[item].astype(BF16)

    pl.semaphore_wait(barrier, parts - 1 + blocks - 1)

    def copy1(slot):
        offset = hop(slot)
        back = slot if slot in (0, parts - 1) else (slot + 1 if slot % 2 else slot - 1)
        return pltpu.make_async_remote_copy(
            src_ref=send1.at[peer(offset)],
            dst_ref=recv1.at[back],
            send_sem=send1_sem.at[slot],
            recv_sem=recv1_sem.at[back],
            device_id={"stab": peer(offset)},
            device_id_type=MESH,
        )

    for slot in range(parts - 1, 0, -1):
        copy1(slot).start()
    recv1[0] = send1[me]

    for index in range(3, INPUTS):
        load(index).wait()
    flip = row(flip_ref)
    gain_attn = row(gain_attn_ref)

    def columns():
        small_ref[...] = jnp.transpose(small_ref[...])
        small_ref[stabs : stabs + 1, :] = small_ref[stabs - 1 : stabs, :]

    def place(first, second):
        low = small_ref[0:rows, second : second + 1]
        flipped = low >= BASE
        coord = small_ref[0:rows, first : first + 1] * BASE + low - jnp.where(flipped, float(BASE), 0.0)
        return coord, jnp.where(flipped, 1.0, -1.0)

    spot = lax.broadcasted_iota(jnp.int32, (rows, coord_rows), 1).astype(F32)

    def look_up(coord):
        picks = [jnp.where(one == spot, 1.0, 0.0) for one in coord]
        return dot(jnp.concatenate(picks, axis=0).astype(BF16), table_ref[...])

    columns()
    for pair in range(rounds // 2):
        base = look_up([place(t, rounds + t)[0] for t in (2 * pair, 2 * pair + 1)])
        for half in range(2):
            t = 2 * pair + half
            for shot in range(shots):
                item = shot * rounds + t
                sign = place(t, rounds * (1 + shot) + t)[1]
                for side in range(2):
                    part = slice(side * LANES, (side + 1) * LANES)
                    start_ref[item, 0:stabs, part] = loose_ref[item, side * rows : side * rows + stabs, :]
                start_ref[item, stabs : stabs + 1, :] = start_ref[item, stabs - 1 : stabs, :]
                start_ref[item] = start_ref[item] + base[half * rows : (half + 1) * rows] + sign * flip

    turned_ref[...] = jnp.transpose(wv_ref[...].astype(F32)).astype(BF16)

    for slots in ARRIVALS:
        for slot in slots:
            if slot:
                pltpu.make_async_remote_copy(
                    src_ref=send1.at[0],
                    dst_ref=recv1.at[slot],
                    send_sem=send1_sem.at[slot],
                    recv_sem=recv1_sem.at[slot],
                    device_id={"stab": peer(1)},
                    device_id_type=MESH,
                ).wait_recv()
            message = recv1[slot].astype(F32)
            index = slot - slots[0]
            for half in range(2):
                part = slice(half * LANES, (half + 1) * LANES)
                mixed_ref[slot * rows : (slot + 1) * rows, part] = message[half * rows : (half + 1) * rows]
            for half in range(2):
                part = slice(half * LANES, (half + 1) * LANES)
                spot_row = half * len(slots) + index
                small_ref[spot_row : spot_row + 1, :] = mixed_ref[slot * rows + stabs : slot * rows + stabs + 1, part]
            mixed_ref[slot * rows + stabs : (slot + 1) * rows, :] = mixed_ref[
                slot * rows + stabs - 1 : (slot + 1) * rows - 1, :
            ]
        columns()
        places = [place(index, len(slots) + index) for index in range(len(slots))]
        sign = jnp.concatenate([jnp.broadcast_to(one[1], (rows, LANES)) for one in places], axis=0)
        sign = jnp.concatenate([sign, sign], axis=1)
        where = slice(slots[0] * rows, (slots[-1] + 1) * rows)
        start = mixed_ref[where, :] + look_up([one[0] for one in places]) + sign * flip
        normed = norm_rows(start, gain_attn).astype(BF16)
        q_ref[where, :] = dot(normed, wq_ref[...]).astype(BF16)
        k_ref[where, :] = dot(normed, wk_ref[...]).astype(BF16)
        n_ref[where, :] = normed
    real = lax.rem(lax.broadcasted_iota(jnp.int32, (1, keys), 1), rows) < stabs
    values = jnp.where(real, dot_t(turned_ref[...], n_ref[...]), 0.0)
    ones = jnp.where(real, jnp.ones((v_ref.shape[1] - HD, keys), F32), 0.0).astype(BF16)
    for head in range(heads):
        v_ref[head, 0:HD, :] = values[head * HD : (head + 1) * HD].astype(BF16)
        v_ref[head, HD:, :] = ones

    def copy2(slot, target):
        return pltpu.make_async_remote_copy(
            src_ref=send2.at[slot],
            dst_ref=recv2.at[me],
            send_sem=send2_sem.at[slot],
            recv_sem=recv2_sem.at[me],
            device_id={"stab": target},
            device_id_type=MESH,
        )

    scale = HD ** (-0.5) * math.log2(math.e)
    done = parts
    last = keys
    for count in COUNTS:
        first = last - count
        query = q_ref[first:last, :].astype(F32)
        head_of = lax.broadcasted_iota(jnp.int32, (count, width), 1) // HD
        for head in range(heads):
            mine = jnp.where(head_of == head, query, 0.0).astype(BF16)
            scores = dot_t(k_ref[...], mine)
            peak = jnp.max(scores, axis=0, keepdims=True)
            weights = jnp.exp2((scores - peak) * scale).astype(BF16)
            both = dot(v_ref[head], weights)
            across_ref[head * HD : (head + 1) * HD, 0:count] = both[:HD] / both[HD : HD + 1]
        mixed_ref[first:last, :] = jnp.transpose(across_ref[:, 0:count])
        while done > 0 and (done - 1) * rows >= first:
            done -= 1
            send2[done] = pack(mixed_ref[done * rows : (done + 1) * rows, :])
            if done:
                copy2(done, peer(hop(done))).start()
        last = first
    recv2[me] = send2[0]

    gain_rec = row(gain_rec_ref)
    for group in range(groups - 1, -1, -1):
        pieces, starts = [], []
        for slot in range(group * GROUP, (group + 1) * GROUP):
            item = peer(hop(slot))
            if slot:
                pltpu.make_async_remote_copy(
                    src_ref=send2.at[0],
                    dst_ref=recv2.at[item],
                    send_sem=send2_sem.at[slot],
                    recv_sem=recv2_sem.at[item],
                    device_id={"stab": peer(1)},
                    device_id_type=MESH,
                ).wait_recv()
            pieces.append(unpack(recv2[item]))
            starts.append(start_ref[item])
        mixed = jnp.concatenate(pieces, axis=0).astype(BF16)
        after = jnp.concatenate(starts, axis=0) + dot(mixed, wo_ref[...])
        rec_in = norm_rows(after, gain_rec).astype(BF16)
        decay = jax.nn.sigmoid(dot(rec_in, wd_ref[...]) + row(bias_ref))
        drive = (1.0 - decay) * dot(rec_in, wi_ref[...])
        for index in range(GROUP):
            item = peer(hop(group * GROUP + index))
            part = slice(index * rows, (index + 1) * rows)
            after_ref[item] = after[part]
            decay_ref[item] = decay[part]
            drive_ref[item] = drive[part]

    for shot in range(shots):
        state = drive_ref[shot * rounds]
        product = decay_ref[shot * rounds]
        for t in range(1, rounds):
            item = shot * rounds + t
            decay = decay_ref[item]
            state = decay * state + drive_ref[item]
            product = product * decay
            drive_ref[item] = state
            decay_ref[item] = product
        for half in range(2):
            part = slice(half * LANES, (half + 1) * LANES)
            send3[2 * shot + half] = jnp.concatenate([product[:, part], state[:, part]], axis=0).astype(BF16)

    chunks = 2 * shots
    step = blocks // chunks
    shift = lax.rem(lax.axis_index("shot"), step)
    my_chunk = lax.div(block, step)
    owner = lax.rem(block, step) == shift

    def copy3(chunk):
        return pltpu.make_async_remote_copy(
            src_ref=send3.at[chunk],
            dst_ref=recv3.at[block],
            send_sem=send3_sem.at[chunk],
            recv_sem=recv3_sem.at[block],
            device_id={"round": chunk * step + shift},
            device_id_type=MESH,
        )

    def copy4(target):
        return pltpu.make_async_remote_copy(
            src_ref=send4.at[target],
            dst_ref=recv4.at[my_chunk],
            send_sem=send4_sem.at[target],
            recv_sem=recv4_sem.at[my_chunk],
            device_id={"round": target},
            device_id_type=MESH,
        )

    for chunk in range(chunks):

        @pl.when(block != chunk * step + shift)
        def _():
            copy3(chunk).start()

        @pl.when(block == chunk * step + shift)
        def _():
            recv3[block] = send3[chunk]

    @pl.when(owner)
    def _():
        entering = jnp.zeros((rows, LANES), F32)
        below = jnp.zeros((send4.shape[1] - rows, LANES), F32)
        for source in range(blocks):
            send4[source] = jnp.concatenate([entering, below], axis=0).astype(BF16)

            @pl.when(block != source)
            def _():
                copy4(source).start()
                pltpu.make_async_remote_copy(
                    src_ref=send3.at[0],
                    dst_ref=recv3.at[source],
                    send_sem=send3_sem.at[0],
                    recv_sem=recv3_sem.at[source],
                    device_id={"round": source},
                    device_id_type=MESH,
                ).wait_recv()

            wide = recv3[source].astype(F32)
            entering = wide[:rows] * entering + wide[rows:]
        recv4[my_chunk] = send4[block]

    for chunk in range(chunks):

        @pl.when(block != chunk * step + shift)
        def _():
            pltpu.make_async_remote_copy(
                src_ref=send4.at[0],
                dst_ref=recv4.at[chunk],
                send_sem=send4_sem.at[0],
                recv_sem=recv4_sem.at[chunk],
                device_id={"round": chunk * step + shift},
                device_id_type=MESH,
            ).wait_recv()

        part = slice((chunk % 2) * LANES, (chunk % 2 + 1) * LANES)
        inc_ref[chunk // 2, :, part] = recv4[chunk].astype(F32)[:rows]

    gain_mlp = row(gain_mlp_ref)

    def finish(group, _):
        hiddens, afters = [], []
        for index in range(FINISH):
            item = group * FINISH + index
            shot = lax.div(item, rounds)
            hiddens.append(drive_ref[item] + decay_ref[item] * inc_ref[shot])
            afters.append(after_ref[item])
        hidden = jnp.concatenate(hiddens, axis=0).astype(BF16)
        after = jnp.concatenate(afters, axis=0) + dot(hidden, wr_ref[...])
        ffn_in = norm_rows(after, gain_mlp).astype(BF16)
        inner = (jax.nn.silu(dot(ffn_in, wg_ref[...])) * dot(ffn_in, wu_ref[...])).astype(BF16)
        states = after + dot(inner, wdown_ref[...])
        for index in range(FINISH):
            item = group * FINISH + index
            first = lax.div(item, rounds) * (stabs * rounds) + lax.rem(item, rounds)
            for half in range(2):
                wide_ref[half, pl.ds(first, stabs, stride=rounds), :] = states[
                    index * rows : index * rows + stabs, half * LANES : (half + 1) * LANES
                ]
        return 0

    lax.fori_loop(0, parts // FINISH, finish, 0)
    for half in range(2):
        out_ref[:, half * LANES : (half + 1) * LANES] = wide_ref[half].astype(BF16)

    for slot in range(1, parts):
        copy1(slot).wait_send()
        copy2(slot, peer(1)).wait_send()
    for chunk in range(chunks):

        @pl.when(block != chunk * step + shift)
        def _():
            copy3(chunk).wait_send()

    for target in range(blocks):

        @pl.when(owner & (block != target))
        def _():
            copy4(target).wait_send()


def body(parts, blocks, *args):
    states_in = args[0]
    shots, rounds, stabs, width = states_in.shape
    assert shots * rounds == parts and sum(COUNTS) == parts * (-(-stabs // 8) * 8)
    assert sum(len(slots) for slots in ARRIVALS) == parts and args[3].shape[0] <= 256 * BASE
    assert len(args) == INPUTS
    rows = -(-stabs // 8) * 8
    flat = (jnp.transpose(states_in, (0, 2, 1, 3)).reshape(-1, width),) + args[1:]
    message = (2 * rows, LANES)
    vmem = pl.BlockSpec(memory_space=pltpu.VMEM)
    dma = pltpu.SemaphoreType.DMA
    result = pl.pallas_call(
        functools.partial(kernel, parts, blocks),
        out_shape=pltpu.VMEM(flat[0].shape, BF16),
        in_specs=[pl.BlockSpec(memory_space=pltpu.HBM)] * len(flat),
        out_specs=vmem,
        scratch_shapes=[pltpu.VMEM(arg.shape, arg.dtype) for arg in flat]
        + [
            pltpu.VMEM((2, flat[0].shape[0], LANES), F32),
            pltpu.VMEM((LANES, LANES), F32),
            pltpu.VMEM((parts,) + message, F32),
            pltpu.VMEM((parts, rows, width), F32),
            pltpu.VMEM((parts,) + message, BF16),
            pltpu.VMEM((parts,) + message, BF16),
            pltpu.VMEM((parts * rows, width), BF16),
            pltpu.VMEM((parts * rows, width), BF16),
            pltpu.VMEM((width // HD, HD + 16, parts * rows), BF16),
            pltpu.VMEM((parts * rows, width), BF16),
            pltpu.VMEM((width, width), BF16),
            pltpu.VMEM((width, max(COUNTS)), F32),
            pltpu.VMEM((parts * rows, width), F32),
            pltpu.VMEM((parts,) + message, BF16),
            pltpu.VMEM((parts,) + message, BF16),
            pltpu.VMEM((parts, rows, width), F32),
            pltpu.VMEM((parts, rows, width), F32),
            pltpu.VMEM((parts, rows, width), F32),
            pltpu.VMEM((2 * shots,) + message, BF16),
            pltpu.VMEM((blocks,) + message, BF16),
            pltpu.VMEM((blocks, -(-rows // 16) * 16, LANES), BF16),
            pltpu.VMEM((2 * shots, -(-rows // 16) * 16, LANES), BF16),
            pltpu.VMEM((shots, rows, width), F32),
            dma((parts,)),
            dma((parts,)),
            dma((parts,)),
            dma((parts,)),
            dma((2 * shots,)),
            dma((blocks,)),
            dma((blocks,)),
            dma((2 * shots,)),
            dma((INPUTS,)),
        ],
        compiler_params=pltpu.CompilerParams(
            collective_id=0, has_side_effects=True, vmem_limit_bytes=58 * 1024 * 1024
        ),
    )(*flat)
    return jnp.transpose(result.reshape(shots, stabs, rounds, width), (0, 2, 1, 3))


def solution(mesh):
    placed = (P("shot", "round", "stab", None), P("shot", "round", "stab"), P("round", "stab")) + (P(),) * 16
    return jax.shard_map(
        functools.partial(body, mesh.shape["stab"], mesh.shape["round"]),
        mesh=mesh,
        in_specs=placed,
        out_specs=P("shot", "round", "stab", None),
        check_vma=False,
    )
```

```python
import functools
import math

import jax
import jax.numpy as jnp
from jax import lax
from jax.experimental import pallas as pl
from jax.experimental.pallas import tpu as pltpu
from jax.sharding import PartitionSpec as P

HD = 32
LANES = 128
GROUP = 4
INPUTS = 19
FINISH = 8
COUNTS = (128, 256, 256)
MESH = pl.DeviceIdType.MESH
F32 = jnp.float32
BF16 = jnp.bfloat16


def dot(left, right):
    return jnp.dot(left, right, preferred_element_type=F32)


def dot_t(left, right):
    return lax.dot_general(left, right, (((1,), (1,)), ((), ())), preferred_element_type=F32)


def norm_rows(values, gain):
    scale = lax.rsqrt(jnp.mean(values * values, axis=-1, keepdims=True) + 1e-05)
    return values * scale * gain


def row(ref):
    return ref[...].astype(F32).reshape(1, -1)


def pack(rows):
    return jnp.concatenate([rows[:, :LANES], rows[:, LANES:]], axis=0).astype(BF16)


def unpack(message):
    wide = message.astype(F32)
    half = wide.shape[0] // 2
    return jnp.concatenate([wide[:half], wide[half:]], axis=1)


def hop(slot):
    return (slot + 1) // 2 if slot % 2 else -(slot // 2)


def kernel(parts, blocks, *refs):
    sources, refs = refs[:INPUTS], refs[INPUTS:]
    out_ref, refs = refs[0], refs[1:]
    operands, refs = refs[:INPUTS], refs[INPUTS:]
    run(parts, blocks, sources, out_ref, operands, *refs)


def run(
    parts,
    blocks,
    sources,
    out_ref,
    operands,
    wide_ref,
    small_ref,
    start_ref,
    send1,
    recv1,
    q_ref,
    k_ref,
    v_ref,
    n_ref,
    turned_ref,
    across_ref,
    mixed_ref,
    send2,
    recv2,
    after_ref,
    decay_ref,
    drive_ref,
    send3,
    recv3,
    send4,
    recv4,
    inc_ref,
    send1_sem,
    recv1_sem,
    send2_sem,
    recv2_sem,
    send3_sem,
    recv3_sem,
    send4_sem,
    recv4_sem,
    load_sem,
):
    (states_ref, bits_ref, coords_ref, table_ref, flip_ref, gain_attn_ref, wq_ref, wk_ref, wv_ref, wo_ref) = operands[:10]
    (gain_rec_ref, wd_ref, bias_ref, wi_ref, wr_ref, gain_mlp_ref, wg_ref, wu_ref, wdown_ref) = operands[10:]
    shots, rounds, stabs = bits_ref.shape
    width = states_ref.shape[1]
    rows = start_ref.shape[1]
    coord_rows = table_ref.shape[0]
    heads = width // HD
    gsize = GROUP * rows
    groups = parts // GROUP
    keys = parts * rows
    me = lax.axis_index("stab")
    block = lax.axis_index("round")

    def peer(offset):
        return lax.rem(me + (offset + parts), parts)

    def load(index):
        return pltpu.make_async_copy(sources[index], operands[index], load_sem.at[index])

    barrier = pltpu.get_barrier_semaphore()
    for offset in range(1, parts):
        pl.semaphore_signal(barrier, inc=1, device_id={"stab": peer(offset)}, device_id_type=MESH)
    for offset in range(1, blocks):
        pl.semaphore_signal(
            barrier, inc=1, device_id={"round": lax.rem(block + offset, blocks)}, device_id_type=MESH
        )

    for index in range(INPUTS):
        load(index).start()

    for index in range(6):
        load(index).wait()
    for half in range(2):
        wide_ref[half] = states_ref[:, half * LANES : (half + 1) * LANES].astype(F32)
    small_ref[...] = jnp.zeros_like(small_ref)
    small_ref[0:rounds, 0:stabs] = coords_ref[...].astype(F32)
    for shot in range(shots):
        first = rounds * (1 + shot)
        small_ref[first : first + rounds, 0:stabs] = bits_ref[shot].astype(F32)
    turned = jnp.transpose(small_ref[...])
    small_ref[...] = turned
    small_ref[stabs : stabs + 1, :] = small_ref[stabs - 1 : stabs, :]
    flip = row(flip_ref)
    gain_attn = row(gain_attn_ref)
    spot = lax.broadcasted_iota(jnp.int32, (rows, coord_rows), 1).astype(F32)
    for pair in range(rounds // 2):
        picks = []
        for t in (2 * pair, 2 * pair + 1):
            picks.append(jnp.where(small_ref[0:rows, t : t + 1] == spot, 1.0, 0.0))
        base = dot(jnp.concatenate(picks, axis=0).astype(BF16), table_ref[...])
        for half in range(2):
            t = 2 * pair + half
            for shot in range(shots):
                item = shot * rounds + t
                lane = rounds * (1 + shot) + t
                where = pl.ds(shot * stabs * rounds + t, stabs, stride=rounds)
                own = jnp.concatenate([wide_ref[0, where, :], wide_ref[1, where, :]], axis=1)
                start_ref[item, 0:stabs, :] = own
                start_ref[item, stabs : stabs + 1, :] = own[stabs - 1 : stabs, :]
                sign = 2.0 * small_ref[0:rows, lane : lane + 1] - 1.0
                start = start_ref[item] + base[half * rows : (half + 1) * rows] + sign * flip
                start_ref[item] = start
                send1[item] = pack(norm_rows(start, gain_attn))

    pl.semaphore_wait(barrier, parts - 1 + blocks - 1)

    def copy1(slot):
        offset = hop(slot)
        back = slot if slot in (0, parts - 1) else (slot + 1 if slot % 2 else slot - 1)
        return pltpu.make_async_remote_copy(
            src_ref=send1.at[peer(offset)],
            dst_ref=recv1.at[back],
            send_sem=send1_sem.at[slot],
            recv_sem=recv1_sem.at[back],
            device_id={"stab": peer(offset)},
            device_id_type=MESH,
        )

    for slot in range(parts - 1, 0, -1):
        copy1(slot).start()
    recv1[0] = send1[me]

    for index in range(6, INPUTS):
        load(index).wait()
    turned_ref[...] = jnp.transpose(wv_ref[...].astype(F32)).astype(BF16)
    for group in range(groups):
        pieces = []
        for slot in range(group * GROUP, (group + 1) * GROUP):
            if slot:
                pltpu.make_async_remote_copy(
                    src_ref=send1.at[0],
                    dst_ref=recv1.at[slot],
                    send_sem=send1_sem.at[slot],
                    recv_sem=recv1_sem.at[slot],
                    device_id={"stab": peer(1)},
                    device_id_type=MESH,
                ).wait_recv()
            pieces.append(unpack(recv1[slot]))
        normed = jnp.concatenate(pieces, axis=0).astype(BF16)
        where = slice(group * gsize, (group + 1) * gsize)
        q_ref[where, :] = dot(normed, wq_ref[...]).astype(BF16)
        k_ref[where, :] = dot(normed, wk_ref[...]).astype(BF16)
        n_ref[where, :] = normed
    real = lax.rem(lax.broadcasted_iota(jnp.int32, (1, keys), 1), rows) < stabs
    values = jnp.where(real, dot_t(turned_ref[...], n_ref[...]), 0.0)
    ones = jnp.where(real, jnp.ones((v_ref.shape[1] - 2 * HD, keys), F32), 0.0).astype(BF16)
    for pair in range(heads // 2):
        v_ref[pair, 0 : 2 * HD, :] = values[2 * HD * pair : 2 * HD * (pair + 1)].astype(BF16)
        v_ref[pair, 2 * HD :, :] = ones

    def copy2(slot, target):
        return pltpu.make_async_remote_copy(
            src_ref=send2.at[slot],
            dst_ref=recv2.at[me],
            send_sem=send2_sem.at[slot],
            recv_sem=recv2_sem.at[me],
            device_id={"stab": target},
            device_id_type=MESH,
        )

    scale = HD ** (-0.5) * math.log2(math.e)
    done = parts
    last = keys
    for count in COUNTS:
        first = last - count
        query = q_ref[first:last, :].astype(F32)
        head_of = lax.broadcasted_iota(jnp.int32, (count, width), 1) // HD
        spread = [jnp.where(head_of == head, query, 0.0) for head in range(heads)]
        scores = dot_t(k_ref[...], jnp.concatenate(spread, axis=0).astype(BF16))
        peak = jnp.max(scores, axis=0, keepdims=True)
        weights = jnp.exp2((scores - peak) * scale).astype(BF16)
        for head in range(0, heads, 2):
            both = dot(v_ref[head // 2], weights[:, head * count : (head + 2) * count])
            for index in range(2):
                piece = both[:, index * count : (index + 1) * count]
                across_ref[(head + index) * HD : (head + index + 1) * HD, 0:count] = (
                    piece[index * HD : (index + 1) * HD] / piece[2 * HD : 2 * HD + 1]
                )
        mixed_ref[first:last, :] = jnp.transpose(across_ref[:, 0:count])
        while done > 0 and (done - 1) * rows >= first:
            done -= 1
            send2[done] = pack(mixed_ref[done * rows : (done + 1) * rows, :])
            if done:
                copy2(done, peer(hop(done))).start()
        last = first
    recv2[me] = send2[0]

    gain_rec = row(gain_rec_ref)
    for group in range(groups - 1, -1, -1):
        pieces, starts = [], []
        for slot in range(group * GROUP, (group + 1) * GROUP):
            item = peer(hop(slot))
            if slot:
                pltpu.make_async_remote_copy(
                    src_ref=send2.at[0],
                    dst_ref=recv2.at[item],
                    send_sem=send2_sem.at[slot],
                    recv_sem=recv2_sem.at[item],
                    device_id={"stab": peer(1)},
                    device_id_type=MESH,
                ).wait_recv()
            pieces.append(unpack(recv2[item]))
            starts.append(start_ref[item])
        mixed = jnp.concatenate(pieces, axis=0).astype(BF16)
        after = jnp.concatenate(starts, axis=0) + dot(mixed, wo_ref[...])
        rec_in = norm_rows(after, gain_rec).astype(BF16)
        decay = jax.nn.sigmoid(dot(rec_in, wd_ref[...]) + row(bias_ref))
        drive = (1.0 - decay) * dot(rec_in, wi_ref[...])
        for index in range(GROUP):
            item = peer(hop(group * GROUP + index))
            part = slice(index * rows, (index + 1) * rows)
            after_ref[item] = after[part]
            decay_ref[item] = decay[part]
            drive_ref[item] = drive[part]

    for shot in range(shots):
        state = drive_ref[shot * rounds]
        product = decay_ref[shot * rounds]
        for t in range(1, rounds):
            item = shot * rounds + t
            decay = decay_ref[item]
            state = decay * state + drive_ref[item]
            product = product * decay
            drive_ref[item] = state
            decay_ref[item] = product
        for half in range(2):
            part = slice(half * LANES, (half + 1) * LANES)
            send3[2 * shot + half] = jnp.concatenate([product[:, part], state[:, part]], axis=0).astype(BF16)

    chunks = 2 * shots
    step = blocks // chunks
    shift = lax.rem(lax.axis_index("shot"), step)
    my_chunk = lax.div(block, step)
    owner = lax.rem(block, step) == shift

    def copy3(chunk):
        return pltpu.make_async_remote_copy(
            src_ref=send3.at[chunk],
            dst_ref=recv3.at[block],
            send_sem=send3_sem.at[chunk],
            recv_sem=recv3_sem.at[block],
            device_id={"round": chunk * step + shift},
            device_id_type=MESH,
        )

    def copy4(target):
        return pltpu.make_async_remote_copy(
            src_ref=send4.at[target],
            dst_ref=recv4.at[my_chunk],
            send_sem=send4_sem.at[target],
            recv_sem=recv4_sem.at[my_chunk],
            device_id={"round": target},
            device_id_type=MESH,
        )

    for chunk in range(chunks):

        @pl.when(block != chunk * step + shift)
        def _():
            copy3(chunk).start()

        @pl.when(block == chunk * step + shift)
        def _():
            recv3[block] = send3[chunk]

    @pl.when(owner)
    def _():
        entering = jnp.zeros((rows, LANES), F32)
        below = jnp.zeros((send4.shape[1] - rows, LANES), F32)
        for source in range(blocks):
            send4[source] = jnp.concatenate([entering, below], axis=0).astype(BF16)

            @pl.when(block != source)
            def _():
                copy4(source).start()
                pltpu.make_async_remote_copy(
                    src_ref=send3.at[0],
                    dst_ref=recv3.at[source],
                    send_sem=send3_sem.at[0],
                    recv_sem=recv3_sem.at[source],
                    device_id={"round": source},
                    device_id_type=MESH,
                ).wait_recv()

            wide = recv3[source].astype(F32)
            entering = wide[:rows] * entering + wide[rows:]
        recv4[my_chunk] = send4[block]

    for chunk in range(chunks):

        @pl.when(block != chunk * step + shift)
        def _():
            pltpu.make_async_remote_copy(
                src_ref=send4.at[0],
                dst_ref=recv4.at[chunk],
                send_sem=send4_sem.at[0],
                recv_sem=recv4_sem.at[chunk],
                device_id={"round": chunk * step + shift},
                device_id_type=MESH,
            ).wait_recv()

        part = slice((chunk % 2) * LANES, (chunk % 2 + 1) * LANES)
        inc_ref[chunk // 2, :, part] = recv4[chunk].astype(F32)[:rows]

    gain_mlp = row(gain_mlp_ref)

    def finish(group, _):
        hiddens, afters = [], []
        for index in range(FINISH):
            item = group * FINISH + index
            shot = lax.div(item, rounds)
            hiddens.append(drive_ref[item] + decay_ref[item] * inc_ref[shot])
            afters.append(after_ref[item])
        hidden = jnp.concatenate(hiddens, axis=0).astype(BF16)
        after = jnp.concatenate(afters, axis=0) + dot(hidden, wr_ref[...])
        ffn_in = norm_rows(after, gain_mlp).astype(BF16)
        inner = (jax.nn.silu(dot(ffn_in, wg_ref[...])) * dot(ffn_in, wu_ref[...])).astype(BF16)
        states = after + dot(inner, wdown_ref[...])
        for index in range(FINISH):
            item = group * FINISH + index
            first = lax.div(item, rounds) * (stabs * rounds) + lax.rem(item, rounds)
            for half in range(2):
                wide_ref[half, pl.ds(first, stabs, stride=rounds), :] = states[
                    index * rows : index * rows + stabs, half * LANES : (half + 1) * LANES
                ]
        return 0

    lax.fori_loop(0, parts // FINISH, finish, 0)
    for half in range(2):
        out_ref[:, half * LANES : (half + 1) * LANES] = wide_ref[half].astype(BF16)

    for slot in range(1, parts):
        copy1(slot).wait_send()
        copy2(slot, peer(1)).wait_send()
    for chunk in range(chunks):

        @pl.when(block != chunk * step + shift)
        def _():
            copy3(chunk).wait_send()

    for target in range(blocks):

        @pl.when(owner & (block != target))
        def _():
            copy4(target).wait_send()


def body(parts, blocks, *args):
    states_in = args[0]
    shots, rounds, stabs, width = states_in.shape
    assert shots * rounds == parts and sum(COUNTS) == parts * (-(-stabs // 8) * 8)
    assert len(args) == INPUTS
    rows = -(-stabs // 8) * 8
    flat = (jnp.transpose(states_in, (0, 2, 1, 3)).reshape(-1, width),) + args[1:]
    message = (2 * rows, LANES)
    vmem = pl.BlockSpec(memory_space=pltpu.VMEM)
    dma = pltpu.SemaphoreType.DMA
    result = pl.pallas_call(
        functools.partial(kernel, parts, blocks),
        out_shape=pltpu.VMEM(flat[0].shape, BF16),
        in_specs=[pl.BlockSpec(memory_space=pltpu.HBM)] * len(flat),
        out_specs=vmem,
        scratch_shapes=[pltpu.VMEM(arg.shape, arg.dtype) for arg in flat]
        + [
            pltpu.VMEM((2, flat[0].shape[0], LANES), F32),
            pltpu.VMEM((LANES, LANES), F32),
            pltpu.VMEM((parts, rows, width), F32),
            pltpu.VMEM((parts,) + message, BF16),
            pltpu.VMEM((parts,) + message, BF16),
            pltpu.VMEM((parts * rows, width), BF16),
            pltpu.VMEM((parts * rows, width), BF16),
            pltpu.VMEM((width // (2 * HD), 2 * HD + 16, parts * rows), BF16),
            pltpu.VMEM((parts * rows, width), BF16),
            pltpu.VMEM((width, width), BF16),
            pltpu.VMEM((width, max(COUNTS)), F32),
            pltpu.VMEM((parts * rows, width), F32),
            pltpu.VMEM((parts,) + message, BF16),
            pltpu.VMEM((parts,) + message, BF16),
            pltpu.VMEM((parts, rows, width), F32),
            pltpu.VMEM((parts, rows, width), F32),
            pltpu.VMEM((parts, rows, width), F32),
            pltpu.VMEM((2 * shots,) + message, BF16),
            pltpu.VMEM((blocks,) + message, BF16),
            pltpu.VMEM((blocks, -(-rows // 16) * 16, LANES), BF16),
            pltpu.VMEM((2 * shots, -(-rows // 16) * 16, LANES), BF16),
            pltpu.VMEM((shots, rows, width), F32),
            dma((parts,)),
            dma((parts,)),
            dma((parts,)),
            dma((parts,)),
            dma((2 * shots,)),
            dma((blocks,)),
            dma((blocks,)),
            dma((2 * shots,)),
            dma((INPUTS,)),
        ],
        compiler_params=pltpu.CompilerParams(
            collective_id=0, has_side_effects=True, vmem_limit_bytes=58 * 1024 * 1024
        ),
    )(*flat)
    return jnp.transpose(result.reshape(shots, stabs, rounds, width), (0, 2, 1, 3))


def solution(mesh):
    placed = (P("shot", "round", "stab", None), P("shot", "round", "stab"), P("round", "stab")) + (P(),) * 16
    return jax.shard_map(
        functools.partial(body, mesh.shape["stab"], mesh.shape["round"]),
        mesh=mesh,
        in_specs=placed,
        out_specs=P("shot", "round", "stab", None),
        check_vma=False,
    )
```

```python
import functools
import math

import jax
import jax.numpy as jnp
from jax import lax
from jax.experimental import pallas as pl
from jax.experimental.pallas import tpu as pltpu
from jax.sharding import PartitionSpec as P

HD = 32
LANES = 128
GROUP = 4
INPUTS = 19
ARRIVALS = ((0, 1, 2, 3), (4, 5, 6, 7), (8, 9, 10, 11), (12, 13), (14, 15))
COUNTS = (128, 256, 256)
MESH = pl.DeviceIdType.MESH
F32 = jnp.float32
BF16 = jnp.bfloat16


def dot(left, right):
    return jnp.dot(left, right, preferred_element_type=F32)


def dot_t(left, right):
    return lax.dot_general(left, right, (((1,), (1,)), ((), ())), preferred_element_type=F32)


def norm_rows(values, gain):
    scale = lax.rsqrt(jnp.mean(values * values, axis=-1, keepdims=True) + 1e-05)
    return values * scale * gain


def row(ref):
    return ref[...].astype(F32).reshape(1, -1)


def pack(rows):
    return jnp.concatenate([rows[:, :LANES], rows[:, LANES:]], axis=0).astype(BF16)


def unpack(message):
    wide = message.astype(F32)
    half = wide.shape[0] // 2
    return jnp.concatenate([wide[:half], wide[half:]], axis=1)


def hop(slot):
    return (slot + 1) // 2 if slot % 2 else -(slot // 2)


def kernel(parts, blocks, *refs):
    sources, refs = refs[:INPUTS], refs[INPUTS:]
    out_ref, refs = refs[0], refs[1:]
    operands, refs = refs[:INPUTS], refs[INPUTS:]
    run(parts, blocks, sources, out_ref, operands, *refs)


def run(
    parts,
    blocks,
    sources,
    out_ref,
    operands,
    wide_ref,
    small_ref,
    start_ref,
    send1,
    recv1,
    q_ref,
    k_ref,
    v_ref,
    n_ref,
    turned_ref,
    across_ref,
    mixed_ref,
    send2,
    recv2,
    after_ref,
    decay_ref,
    drive_ref,
    send3,
    recv3,
    send4,
    recv4,
    send1_sem,
    recv1_sem,
    send2_sem,
    recv2_sem,
    send3_sem,
    recv3_sem,
    send4_sem,
    recv4_sem,
    load_sem,
):
    (states_ref, bits_ref, coords_ref, table_ref, flip_ref, gain_attn_ref, wq_ref, wk_ref, wv_ref, wo_ref) = operands[:10]
    (gain_rec_ref, wd_ref, bias_ref, wi_ref, wr_ref, gain_mlp_ref, wg_ref, wu_ref, wdown_ref) = operands[10:]
    shots, rounds, stabs = bits_ref.shape
    width = states_ref.shape[1]
    rows = start_ref.shape[1]
    coord_rows = table_ref.shape[0]
    heads = width // HD
    gsize = GROUP * rows
    groups = parts // GROUP
    keys = parts * rows
    me = lax.axis_index("stab")
    block = lax.axis_index("round")

    def peer(offset):
        return lax.rem(me + (offset + parts), parts)

    def load(index):
        return pltpu.make_async_copy(sources[index], operands[index], load_sem.at[index])

    barrier = pltpu.get_barrier_semaphore()
    for offset in range(1, parts):
        pl.semaphore_signal(barrier, inc=1, device_id={"stab": peer(offset)}, device_id_type=MESH)
    for offset in range(1, blocks):
        pl.semaphore_signal(
            barrier, inc=1, device_id={"round": lax.rem(block + offset, blocks)}, device_id_type=MESH
        )

    for index in range(INPUTS):
        load(index).start()

    for index in range(6):
        load(index).wait()
    for half in range(2):
        wide_ref[half] = states_ref[:, half * LANES : (half + 1) * LANES].astype(F32)
    small_ref[...] = jnp.zeros_like(small_ref)
    small_ref[0:rounds, 0:stabs] = coords_ref[...].astype(F32)
    for shot in range(shots):
        first = rounds * (1 + shot)
        small_ref[first : first + rounds, 0:stabs] = bits_ref[shot].astype(F32)
    turned = jnp.transpose(small_ref[...])
    small_ref[...] = turned
    small_ref[stabs : stabs + 1, :] = small_ref[stabs - 1 : stabs, :]
    flip = row(flip_ref)
    gain_attn = row(gain_attn_ref)
    spot = lax.broadcasted_iota(jnp.int32, (rows, coord_rows), 1).astype(F32)
    for pair in range(rounds // 2):
        picks = []
        for t in (2 * pair, 2 * pair + 1):
            picks.append(jnp.where(small_ref[0:rows, t : t + 1] == spot, 1.0, 0.0))
        base = dot(jnp.concatenate(picks, axis=0).astype(BF16), table_ref[...])
        for half in range(2):
            t = 2 * pair + half
            for shot in range(shots):
                item = shot * rounds + t
                lane = rounds * (1 + shot) + t
                where = pl.ds(shot * stabs * rounds + t, stabs, stride=rounds)
                own = jnp.concatenate([wide_ref[0, where, :], wide_ref[1, where, :]], axis=1)
                start_ref[item, 0:stabs, :] = own
                start_ref[item, stabs : stabs + 1, :] = own[stabs - 1 : stabs, :]
                sign = 2.0 * small_ref[0:rows, lane : lane + 1] - 1.0
                start = start_ref[item] + base[half * rows : (half + 1) * rows] + sign * flip
                start_ref[item] = start
                send1[item] = pack(norm_rows(start, gain_attn))

    pl.semaphore_wait(barrier, parts - 1 + blocks - 1)

    def copy1(slot):
        offset = hop(slot)
        back = slot if slot in (0, parts - 1) else (slot + 1 if slot % 2 else slot - 1)
        return pltpu.make_async_remote_copy(
            src_ref=send1.at[peer(offset)],
            dst_ref=recv1.at[back],
            send_sem=send1_sem.at[slot],
            recv_sem=recv1_sem.at[back],
            device_id={"stab": peer(offset)},
            device_id_type=MESH,
        )

    for slot in range(1, parts):
        copy1(slot).start()
    recv1[0] = send1[me]

    for index in range(6, INPUTS):
        load(index).wait()
    turned_ref[...] = jnp.transpose(wv_ref[...].astype(F32)).astype(BF16)
    for slots in ARRIVALS:
        pieces = []
        for slot in slots:
            if slot:
                pltpu.make_async_remote_copy(
                    src_ref=send1.at[0],
                    dst_ref=recv1.at[slot],
                    send_sem=send1_sem.at[slot],
                    recv_sem=recv1_sem.at[slot],
                    device_id={"stab": peer(1)},
                    device_id_type=MESH,
                ).wait_recv()
            pieces.append(unpack(recv1[slot]))
        normed = jnp.concatenate(pieces, axis=0).astype(BF16)
        where = slice(slots[0] * rows, (slots[-1] + 1) * rows)
        q_ref[where, :] = dot(normed, wq_ref[...]).astype(BF16)
        k_ref[where, :] = dot(normed, wk_ref[...]).astype(BF16)
        n_ref[where, :] = normed
    real = lax.rem(lax.broadcasted_iota(jnp.int32, (1, keys), 1), rows) < stabs
    values = jnp.where(real, dot_t(turned_ref[...], n_ref[...]), 0.0)
    ones = jnp.where(real, jnp.ones((v_ref.shape[1] - 2 * HD, keys), F32), 0.0).astype(BF16)
    for pair in range(heads // 2):
        v_ref[pair, 0 : 2 * HD, :] = values[2 * HD * pair : 2 * HD * (pair + 1)].astype(BF16)
        v_ref[pair, 2 * HD :, :] = ones

    def copy2(slot, target):
        return pltpu.make_async_remote_copy(
            src_ref=send2.at[slot],
            dst_ref=recv2.at[me],
            send_sem=send2_sem.at[slot],
            recv_sem=recv2_sem.at[me],
            device_id={"stab": target},
            device_id_type=MESH,
        )

    scale = HD ** (-0.5) * math.log2(math.e)
    done = parts
    last = keys
    for count in COUNTS:
        first = last - count
        query = q_ref[first:last, :].astype(F32)
        head_of = lax.broadcasted_iota(jnp.int32, (count, width), 1) // HD
        spread = [jnp.where(head_of == head, query, 0.0) for head in range(heads)]
        scores = dot_t(k_ref[...], jnp.concatenate(spread, axis=0).astype(BF16))
        peak = jnp.max(scores, axis=0, keepdims=True)
        weights = jnp.exp2((scores - peak) * scale).astype(BF16)
        for head in range(0, heads, 2):
            both = dot(v_ref[head // 2], weights[:, head * count : (head + 2) * count])
            for index in range(2):
                piece = both[:, index * count : (index + 1) * count]
                across_ref[(head + index) * HD : (head + index + 1) * HD, 0:count] = (
                    piece[index * HD : (index + 1) * HD] / piece[2 * HD : 2 * HD + 1]
                )
        mixed_ref[first:last, :] = jnp.transpose(across_ref[:, 0:count])
        while done > 0 and (done - 1) * rows >= first:
            done -= 1
            send2[done] = pack(mixed_ref[done * rows : (done + 1) * rows, :])
            if done:
                copy2(done, peer(hop(done))).start()
        last = first
    recv2[me] = send2[0]

    gain_rec = row(gain_rec_ref)
    for group in range(groups - 1, -1, -1):
        pieces, starts = [], []
        for slot in range(group * GROUP, (group + 1) * GROUP):
            item = peer(hop(slot))
            if slot:
                pltpu.make_async_remote_copy(
                    src_ref=send2.at[0],
                    dst_ref=recv2.at[item],
                    send_sem=send2_sem.at[slot],
                    recv_sem=recv2_sem.at[item],
                    device_id={"stab": peer(1)},
                    device_id_type=MESH,
                ).wait_recv()
            pieces.append(unpack(recv2[item]))
            starts.append(start_ref[item])
        mixed = jnp.concatenate(pieces, axis=0).astype(BF16)
        after = jnp.concatenate(starts, axis=0) + dot(mixed, wo_ref[...])
        rec_in = norm_rows(after, gain_rec).astype(BF16)
        decay = jax.nn.sigmoid(dot(rec_in, wd_ref[...]) + row(bias_ref))
        drive = (1.0 - decay) * dot(rec_in, wi_ref[...])
        for index in range(GROUP):
            item = peer(hop(group * GROUP + index))
            part = slice(index * rows, (index + 1) * rows)
            after_ref[item] = after[part]
            decay_ref[item] = decay[part]
            drive_ref[item] = drive[part]

    chunks = 2 * shots
    step = blocks // chunks
    shift = lax.rem(lax.axis_index("shot"), step)
    my_chunk = lax.div(block, step)
    owner = lax.rem(block, step) == shift

    def copy3(chunk):
        return pltpu.make_async_remote_copy(
            src_ref=send3.at[chunk],
            dst_ref=recv3.at[block],
            send_sem=send3_sem.at[chunk],
            recv_sem=recv3_sem.at[block],
            device_id={"round": chunk * step + shift},
            device_id_type=MESH,
        )

    def copy4(target):
        return pltpu.make_async_remote_copy(
            src_ref=send4.at[target],
            dst_ref=recv4.at[my_chunk],
            send_sem=send4_sem.at[target],
            recv_sem=recv4_sem.at[my_chunk],
            device_id={"round": target},
            device_id_type=MESH,
        )

    for shot in range(shots):
        state = drive_ref[shot * rounds]
        product = decay_ref[shot * rounds]
        for t in range(1, rounds):
            item = shot * rounds + t
            decay = decay_ref[item]
            state = decay * state + drive_ref[item]
            product = product * decay
            drive_ref[item] = state
            decay_ref[item] = product
        for half in range(2):
            part = slice(half * LANES, (half + 1) * LANES)
            send3[2 * shot + half] = jnp.concatenate([product[:, part], state[:, part]], axis=0).astype(BF16)
            chunk = 2 * shot + half

            @pl.when(block != chunk * step + shift)
            def _():
                copy3(chunk).start()

            @pl.when(block == chunk * step + shift)
            def _():
                recv3[block] = send3[chunk]

    @pl.when(owner)
    def _():
        entering = jnp.zeros((rows, LANES), F32)
        below = jnp.zeros((send4.shape[1] - rows, LANES), F32)
        for source in range(blocks):
            send4[source] = jnp.concatenate([entering, below], axis=0).astype(BF16)

            @pl.when(block != source)
            def _():
                copy4(source).start()
                pltpu.make_async_remote_copy(
                    src_ref=send3.at[0],
                    dst_ref=recv3.at[source],
                    send_sem=send3_sem.at[0],
                    recv_sem=recv3_sem.at[source],
                    device_id={"round": source},
                    device_id_type=MESH,
                ).wait_recv()

            wide = recv3[source].astype(F32)
            entering = wide[:rows] * entering + wide[rows:]
        recv4[my_chunk] = send4[block]

    gain_mlp = row(gain_mlp_ref)
    for shot in range(shots):
        halves = []
        for chunk in (2 * shot, 2 * shot + 1):

            @pl.when(block != chunk * step + shift)
            def _():
                pltpu.make_async_remote_copy(
                    src_ref=send4.at[0],
                    dst_ref=recv4.at[chunk],
                    send_sem=send4_sem.at[0],
                    recv_sem=recv4_sem.at[chunk],
                    device_id={"round": chunk * step + shift},
                    device_id_type=MESH,
                ).wait_recv()

            halves.append(recv4[chunk].astype(F32)[:rows])
        entering = jnp.concatenate(halves, axis=1)
        items = range(shot * rounds, (shot + 1) * rounds)
        hidden = [drive_ref[item] + decay_ref[item] * entering for item in items]
        after = jnp.concatenate([after_ref[item] for item in items], axis=0)
        after = after + dot(jnp.concatenate(hidden, axis=0).astype(BF16), wr_ref[...])
        ffn_in = norm_rows(after, gain_mlp).astype(BF16)
        inner = (jax.nn.silu(dot(ffn_in, wg_ref[...])) * dot(ffn_in, wu_ref[...])).astype(BF16)
        states = after + dot(inner, wdown_ref[...])
        for t in range(rounds):
            where = pl.ds(shot * stabs * rounds + t, stabs, stride=rounds)
            for half in range(2):
                wide_ref[half, where, :] = states[t * rows : t * rows + stabs, half * LANES : (half + 1) * LANES]
    for half in range(2):
        out_ref[:, half * LANES : (half + 1) * LANES] = wide_ref[half].astype(BF16)

    for slot in range(1, parts):
        copy1(slot).wait_send()
        copy2(slot, peer(1)).wait_send()
    for chunk in range(chunks):

        @pl.when(block != chunk * step + shift)
        def _():
            copy3(chunk).wait_send()

    for target in range(blocks):

        @pl.when(owner & (block != target))
        def _():
            copy4(target).wait_send()


def body(parts, blocks, *args):
    states_in = args[0]
    shots, rounds, stabs, width = states_in.shape
    assert shots * rounds == parts and sum(map(len, ARRIVALS)) == parts
    assert sum(COUNTS) == parts * (-(-stabs // 8) * 8)
    assert len(args) == INPUTS
    rows = -(-stabs // 8) * 8
    flat = (jnp.transpose(states_in, (0, 2, 1, 3)).reshape(-1, width),) + args[1:]
    message = (2 * rows, LANES)
    vmem = pl.BlockSpec(memory_space=pltpu.VMEM)
    dma = pltpu.SemaphoreType.DMA
    result = pl.pallas_call(
        functools.partial(kernel, parts, blocks),
        out_shape=pltpu.VMEM(flat[0].shape, BF16),
        in_specs=[pl.BlockSpec(memory_space=pltpu.HBM)] * len(flat),
        out_specs=vmem,
        scratch_shapes=[pltpu.VMEM(arg.shape, arg.dtype) for arg in flat]
        + [
            pltpu.VMEM((2, flat[0].shape[0], LANES), F32),
            pltpu.VMEM((LANES, LANES), F32),
            pltpu.VMEM((parts, rows, width), F32),
            pltpu.VMEM((parts,) + message, BF16),
            pltpu.VMEM((parts,) + message, BF16),
            pltpu.VMEM((parts * rows, width), BF16),
            pltpu.VMEM((parts * rows, width), BF16),
            pltpu.VMEM((width // (2 * HD), 2 * HD + 16, parts * rows), BF16),
            pltpu.VMEM((parts * rows, width), BF16),
            pltpu.VMEM((width, width), BF16),
            pltpu.VMEM((width, max(COUNTS)), F32),
            pltpu.VMEM((parts * rows, width), F32),
            pltpu.VMEM((parts,) + message, BF16),
            pltpu.VMEM((parts,) + message, BF16),
            pltpu.VMEM((parts, rows, width), F32),
            pltpu.VMEM((parts, rows, width), F32),
            pltpu.VMEM((parts, rows, width), F32),
            pltpu.VMEM((2 * shots,) + message, BF16),
            pltpu.VMEM((blocks,) + message, BF16),
            pltpu.VMEM((blocks, -(-rows // 16) * 16, LANES), BF16),
            pltpu.VMEM((2 * shots, -(-rows // 16) * 16, LANES), BF16),
            dma((parts,)),
            dma((parts,)),
            dma((parts,)),
            dma((parts,)),
            dma((2 * shots,)),
            dma((blocks,)),
            dma((blocks,)),
            dma((2 * shots,)),
            dma((INPUTS,)),
        ],
        compiler_params=pltpu.CompilerParams(
            collective_id=0, has_side_effects=True, vmem_limit_bytes=58 * 1024 * 1024
        ),
    )(*flat)
    return jnp.transpose(result.reshape(shots, stabs, rounds, width), (0, 2, 1, 3))


def solution(mesh):
    placed = (P("shot", "round", "stab", None), P("shot", "round", "stab"), P("round", "stab")) + (P(),) * 16
    return jax.shard_map(
        functools.partial(body, mesh.shape["stab"], mesh.shape["round"]),
        mesh=mesh,
        in_specs=placed,
        out_specs=P("shot", "round", "stab", None),
        check_vma=False,
    )
```

```python
import functools
import math

import jax
import jax.numpy as jnp
from jax import lax
from jax.experimental import pallas as pl
from jax.experimental.pallas import tpu as pltpu
from jax.sharding import PartitionSpec as P

HD = 32
LANES = 128
INPUTS = 19
ARRIVALS = ((0, 1, 2, 3), (4, 5, 6, 7), (8, 9, 10, 11), (12, 13), (14, 15))
COUNTS = (128, 256, 256)
GATES = ((12, 13, 14, 15), (8, 9, 10, 11), (4, 5, 6, 7), (2, 3), (0, 1))
MESH = pl.DeviceIdType.MESH
F32 = jnp.float32
BF16 = jnp.bfloat16


def dot(left, right):
    return jnp.dot(left, right, preferred_element_type=F32)


def dot_t(left, right):
    return lax.dot_general(left, right, (((1,), (1,)), ((), ())), preferred_element_type=F32)


def norm_rows(values, gain):
    scale = lax.rsqrt(jnp.mean(values * values, axis=-1, keepdims=True) + 1e-05)
    return values * scale * gain


def row(ref):
    return ref[...].astype(F32).reshape(1, -1)


def pack(rows):
    return jnp.concatenate([rows[:, :LANES], rows[:, LANES:]], axis=0).astype(BF16)


def unpack(message):
    wide = message.astype(F32)
    half = wide.shape[0] // 2
    return jnp.concatenate([wide[:half], wide[half:]], axis=1)


def hop(slot):
    return (slot + 1) // 2 if slot % 2 else -(slot // 2)


def kernel(parts, blocks, *refs):
    sources, refs = refs[:INPUTS], refs[INPUTS:]
    out_ref, refs = refs[0], refs[1:]
    operands, refs = refs[:INPUTS], refs[INPUTS:]
    run(parts, blocks, sources, out_ref, operands, *refs)


def run(
    parts,
    blocks,
    sources,
    out_ref,
    operands,
    wide_ref,
    small_ref,
    start_ref,
    send1,
    recv1,
    q_ref,
    k_ref,
    v_ref,
    n_ref,
    turned_ref,
    across_ref,
    mixed_ref,
    send2,
    recv2,
    after_ref,
    decay_ref,
    drive_ref,
    send3,
    recv3,
    send4,
    recv4,
    send1_sem,
    recv1_sem,
    send2_sem,
    recv2_sem,
    send3_sem,
    recv3_sem,
    send4_sem,
    recv4_sem,
    load_sem,
):
    (states_ref, bits_ref, coords_ref, table_ref, flip_ref, gain_attn_ref, wq_ref, wk_ref, wv_ref, wo_ref) = operands[:10]
    (gain_rec_ref, wd_ref, bias_ref, wi_ref, wr_ref, gain_mlp_ref, wg_ref, wu_ref, wdown_ref) = operands[10:]
    shots, rounds, stabs = bits_ref.shape
    width = states_ref.shape[1]
    rows = start_ref.shape[1]
    coord_rows = table_ref.shape[0]
    heads = width // HD
    keys = parts * rows
    me = lax.axis_index("stab")
    block = lax.axis_index("round")

    def peer(offset):
        return lax.rem(me + (offset + parts), parts)

    def load(index):
        return pltpu.make_async_copy(sources[index], operands[index], load_sem.at[index])

    barrier = pltpu.get_barrier_semaphore()
    for offset in range(1, parts):
        pl.semaphore_signal(barrier, inc=1, device_id={"stab": peer(offset)}, device_id_type=MESH)
    for offset in range(1, blocks):
        pl.semaphore_signal(
            barrier, inc=1, device_id={"round": lax.rem(block + offset, blocks)}, device_id_type=MESH
        )

    for index in range(INPUTS):
        load(index).start()

    for index in range(6):
        load(index).wait()
    for half in range(2):
        wide_ref[half] = states_ref[:, half * LANES : (half + 1) * LANES].astype(F32)
    small_ref[...] = jnp.zeros_like(small_ref)
    small_ref[0:rounds, 0:stabs] = coords_ref[...].astype(F32)
    for shot in range(shots):
        first = rounds * (1 + shot)
        small_ref[first : first + rounds, 0:stabs] = bits_ref[shot].astype(F32)
    turned = jnp.transpose(small_ref[...])
    small_ref[...] = turned
    small_ref[stabs : stabs + 1, :] = small_ref[stabs - 1 : stabs, :]
    flip = row(flip_ref)
    gain_attn = row(gain_attn_ref)
    spot = lax.broadcasted_iota(jnp.int32, (rows, coord_rows), 1).astype(F32)
    for pair in range(rounds // 2):
        picks = []
        for t in (2 * pair, 2 * pair + 1):
            picks.append(jnp.where(small_ref[0:rows, t : t + 1] == spot, 1.0, 0.0))
        base = dot(jnp.concatenate(picks, axis=0).astype(BF16), table_ref[...])
        for half in range(2):
            t = 2 * pair + half
            for shot in range(shots):
                item = shot * rounds + t
                lane = rounds * (1 + shot) + t
                where = pl.ds(shot * stabs * rounds + t, stabs, stride=rounds)
                own = jnp.concatenate([wide_ref[0, where, :], wide_ref[1, where, :]], axis=1)
                start_ref[item, 0:stabs, :] = own
                start_ref[item, stabs : stabs + 1, :] = own[stabs - 1 : stabs, :]
                sign = 2.0 * small_ref[0:rows, lane : lane + 1] - 1.0
                start = start_ref[item] + base[half * rows : (half + 1) * rows] + sign * flip
                start_ref[item] = start
                send1[item] = pack(norm_rows(start, gain_attn))

    pl.semaphore_wait(barrier, parts - 1 + blocks - 1)

    def copy1(slot):
        offset = hop(slot)
        back = slot if slot in (0, parts - 1) else (slot + 1 if slot % 2 else slot - 1)
        return pltpu.make_async_remote_copy(
            src_ref=send1.at[peer(offset)],
            dst_ref=recv1.at[back],
            send_sem=send1_sem.at[slot],
            recv_sem=recv1_sem.at[back],
            device_id={"stab": peer(offset)},
            device_id_type=MESH,
        )

    for slot in range(1, parts):
        copy1(slot).start()
    recv1[0] = send1[me]

    for index in range(6, INPUTS):
        load(index).wait()
    turned_ref[...] = jnp.transpose(wv_ref[...].astype(F32)).astype(BF16)
    def turn(first, last):
        lane = first + lax.broadcasted_iota(jnp.int32, (1, last - first), 1)
        real = lax.rem(lane, rows) < stabs
        values = jnp.where(real, dot_t(turned_ref[...], n_ref[first:last, :]), 0.0)
        ones = jnp.where(real, jnp.ones((v_ref.shape[1] - 2 * HD, last - first), F32), 0.0).astype(BF16)
        for pair in range(heads // 2):
            v_ref[pair, 0 : 2 * HD, first:last] = values[2 * HD * pair : 2 * HD * (pair + 1)].astype(BF16)
            v_ref[pair, 2 * HD :, first:last] = ones

    ready = 0
    for slots in ARRIVALS:
        pieces = []
        for slot in slots:
            if slot:
                pltpu.make_async_remote_copy(
                    src_ref=send1.at[0],
                    dst_ref=recv1.at[slot],
                    send_sem=send1_sem.at[slot],
                    recv_sem=recv1_sem.at[slot],
                    device_id={"stab": peer(1)},
                    device_id_type=MESH,
                ).wait_recv()
            pieces.append(unpack(recv1[slot]))
        normed = jnp.concatenate(pieces, axis=0).astype(BF16)
        where = slice(slots[0] * rows, (slots[-1] + 1) * rows)
        q_ref[where, :] = dot(normed, wq_ref[...]).astype(BF16)
        k_ref[where, :] = dot(normed, wk_ref[...]).astype(BF16)
        n_ref[where, :] = normed
        upto = (slots[-1] + 1) * rows // LANES * LANES
        if upto - ready >= 2 * LANES or upto == keys:
            turn(ready, upto)
            ready = upto

    def copy2(slot, target):
        return pltpu.make_async_remote_copy(
            src_ref=send2.at[slot],
            dst_ref=recv2.at[me],
            send_sem=send2_sem.at[slot],
            recv_sem=recv2_sem.at[me],
            device_id={"stab": target},
            device_id_type=MESH,
        )

    scale = HD ** (-0.5) * math.log2(math.e)
    done = parts
    last = keys
    for count in COUNTS:
        first = last - count
        query = q_ref[first:last, :].astype(F32)
        head_of = lax.broadcasted_iota(jnp.int32, (count, width), 1) // HD
        spread = [jnp.where(head_of == head, query, 0.0) for head in range(heads)]
        scores = dot_t(k_ref[...], jnp.concatenate(spread, axis=0).astype(BF16))
        peak = jnp.max(scores, axis=0, keepdims=True)
        weights = jnp.exp2((scores - peak) * scale).astype(BF16)
        for head in range(0, heads, 2):
            both = dot(v_ref[head // 2], weights[:, head * count : (head + 2) * count])
            for index in range(2):
                piece = both[:, index * count : (index + 1) * count]
                across_ref[(head + index) * HD : (head + index + 1) * HD, 0:count] = (
                    piece[index * HD : (index + 1) * HD] / piece[2 * HD : 2 * HD + 1]
                )
        mixed_ref[first:last, :] = jnp.transpose(across_ref[:, 0:count])
        while done > 0 and (done - 1) * rows >= first:
            done -= 1
            send2[done] = pack(mixed_ref[done * rows : (done + 1) * rows, :])
            if done:
                copy2(done, peer(hop(done))).start()
        last = first
    recv2[me] = send2[0]

    gain_rec = row(gain_rec_ref)
    for slots in GATES:
        pieces, starts = [], []
        for slot in slots:
            item = peer(hop(slot))
            if slot:
                pltpu.make_async_remote_copy(
                    src_ref=send2.at[0],
                    dst_ref=recv2.at[item],
                    send_sem=send2_sem.at[slot],
                    recv_sem=recv2_sem.at[item],
                    device_id={"stab": peer(1)},
                    device_id_type=MESH,
                ).wait_recv()
            pieces.append(unpack(recv2[item]))
            starts.append(start_ref[item])
        mixed = jnp.concatenate(pieces, axis=0).astype(BF16)
        after = jnp.concatenate(starts, axis=0) + dot(mixed, wo_ref[...])
        rec_in = norm_rows(after, gain_rec).astype(BF16)
        decay = jax.nn.sigmoid(dot(rec_in, wd_ref[...]) + row(bias_ref))
        drive = (1.0 - decay) * dot(rec_in, wi_ref[...])
        for index, slot in enumerate(slots):
            item = peer(hop(slot))
            part = slice(index * rows, (index + 1) * rows)
            after_ref[item] = after[part]
            decay_ref[item] = decay[part]
            drive_ref[item] = drive[part]

    chunks = 2 * shots
    step = blocks // chunks
    shift = lax.rem(lax.axis_index("shot"), step)
    my_chunk = lax.div(block, step)
    owner = lax.rem(block, step) == shift

    def copy3(chunk):
        return pltpu.make_async_remote_copy(
            src_ref=send3.at[chunk],
            dst_ref=recv3.at[block],
            send_sem=send3_sem.at[chunk],
            recv_sem=recv3_sem.at[block],
            device_id={"round": chunk * step + shift},
            device_id_type=MESH,
        )

    def copy4(target):
        return pltpu.make_async_remote_copy(
            src_ref=send4.at[target],
            dst_ref=recv4.at[my_chunk],
            send_sem=send4_sem.at[target],
            recv_sem=recv4_sem.at[my_chunk],
            device_id={"round": target},
            device_id_type=MESH,
        )

    for shot in range(shots):
        state = drive_ref[shot * rounds]
        product = decay_ref[shot * rounds]
        for t in range(1, rounds):
            item = shot * rounds + t
            decay = decay_ref[item]
            state = decay * state + drive_ref[item]
            product = product * decay
            drive_ref[item] = state
            decay_ref[item] = product
        for half in range(2):
            part = slice(half * LANES, (half + 1) * LANES)
            send3[2 * shot + half] = jnp.concatenate([product[:, part], state[:, part]], axis=0).astype(BF16)
            chunk = 2 * shot + half

            @pl.when(block != chunk * step + shift)
            def _():
                copy3(chunk).start()

            @pl.when(block == chunk * step + shift)
            def _():
                recv3[block] = send3[chunk]

    @pl.when(owner)
    def _():
        entering = jnp.zeros((rows, LANES), F32)
        below = jnp.zeros((send4.shape[1] - rows, LANES), F32)
        for source in range(blocks):
            send4[source] = jnp.concatenate([entering, below], axis=0).astype(BF16)

            @pl.when(block != source)
            def _():
                copy4(source).start()
                pltpu.make_async_remote_copy(
                    src_ref=send3.at[0],
                    dst_ref=recv3.at[source],
                    send_sem=send3_sem.at[0],
                    recv_sem=recv3_sem.at[source],
                    device_id={"round": source},
                    device_id_type=MESH,
                ).wait_recv()

            wide = recv3[source].astype(F32)
            entering = wide[:rows] * entering + wide[rows:]
        recv4[my_chunk] = send4[block]

    gain_mlp = row(gain_mlp_ref)
    for shot in range(shots):
        halves = []
        for chunk in (2 * shot, 2 * shot + 1):

            @pl.when(block != chunk * step + shift)
            def _():
                pltpu.make_async_remote_copy(
                    src_ref=send4.at[0],
                    dst_ref=recv4.at[chunk],
                    send_sem=send4_sem.at[0],
                    recv_sem=recv4_sem.at[chunk],
                    device_id={"round": chunk * step + shift},
                    device_id_type=MESH,
                ).wait_recv()

            halves.append(recv4[chunk].astype(F32)[:rows])
        entering = jnp.concatenate(halves, axis=1)
        items = range(shot * rounds, (shot + 1) * rounds)
        hidden = [drive_ref[item] + decay_ref[item] * entering for item in items]
        after = jnp.concatenate([after_ref[item] for item in items], axis=0)
        after = after + dot(jnp.concatenate(hidden, axis=0).astype(BF16), wr_ref[...])
        ffn_in = norm_rows(after, gain_mlp).astype(BF16)
        inner = (jax.nn.silu(dot(ffn_in, wg_ref[...])) * dot(ffn_in, wu_ref[...])).astype(BF16)
        states = after + dot(inner, wdown_ref[...])
        for t in range(rounds):
            where = pl.ds(shot * stabs * rounds + t, stabs, stride=rounds)
            for half in range(2):
                wide_ref[half, where, :] = states[t * rows : t * rows + stabs, half * LANES : (half + 1) * LANES]
    for half in range(2):
        out_ref[:, half * LANES : (half + 1) * LANES] = wide_ref[half].astype(BF16)

    for slot in range(1, parts):
        copy1(slot).wait_send()
        copy2(slot, peer(1)).wait_send()
    for chunk in range(chunks):

        @pl.when(block != chunk * step + shift)
        def _():
            copy3(chunk).wait_send()

    for target in range(blocks):

        @pl.when(owner & (block != target))
        def _():
            copy4(target).wait_send()


def body(parts, blocks, *args):
    states_in = args[0]
    shots, rounds, stabs, width = states_in.shape
    assert shots * rounds == parts and sum(map(len, ARRIVALS)) == parts
    assert sum(map(len, GATES)) == parts and sum(COUNTS) == parts * (-(-stabs // 8) * 8)
    assert len(args) == INPUTS
    rows = -(-stabs // 8) * 8
    flat = (jnp.transpose(states_in, (0, 2, 1, 3)).reshape(-1, width),) + args[1:]
    message = (2 * rows, LANES)
    vmem = pl.BlockSpec(memory_space=pltpu.VMEM)
    dma = pltpu.SemaphoreType.DMA
    result = pl.pallas_call(
        functools.partial(kernel, parts, blocks),
        out_shape=pltpu.VMEM(flat[0].shape, BF16),
        in_specs=[pl.BlockSpec(memory_space=pltpu.HBM)] * len(flat),
        out_specs=vmem,
        scratch_shapes=[pltpu.VMEM(arg.shape, arg.dtype) for arg in flat]
        + [
            pltpu.VMEM((2, flat[0].shape[0], LANES), F32),
            pltpu.VMEM((LANES, LANES), F32),
            pltpu.VMEM((parts, rows, width), F32),
            pltpu.VMEM((parts,) + message, BF16),
            pltpu.VMEM((parts,) + message, BF16),
            pltpu.VMEM((parts * rows, width), BF16),
            pltpu.VMEM((parts * rows, width), BF16),
            pltpu.VMEM((width // (2 * HD), 2 * HD + 16, parts * rows), BF16),
            pltpu.VMEM((parts * rows, width), BF16),
            pltpu.VMEM((width, width), BF16),
            pltpu.VMEM((width, max(COUNTS)), F32),
            pltpu.VMEM((parts * rows, width), F32),
            pltpu.VMEM((parts,) + message, BF16),
            pltpu.VMEM((parts,) + message, BF16),
            pltpu.VMEM((parts, rows, width), F32),
            pltpu.VMEM((parts, rows, width), F32),
            pltpu.VMEM((parts, rows, width), F32),
            pltpu.VMEM((2 * shots,) + message, BF16),
            pltpu.VMEM((blocks,) + message, BF16),
            pltpu.VMEM((blocks, -(-rows // 16) * 16, LANES), BF16),
            pltpu.VMEM((2 * shots, -(-rows // 16) * 16, LANES), BF16),
            dma((parts,)),
            dma((parts,)),
            dma((parts,)),
            dma((parts,)),
            dma((2 * shots,)),
            dma((blocks,)),
            dma((blocks,)),
            dma((2 * shots,)),
            dma((INPUTS,)),
        ],
        compiler_params=pltpu.CompilerParams(
            collective_id=0, has_side_effects=True, vmem_limit_bytes=58 * 1024 * 1024
        ),
    )(*flat)
    return jnp.transpose(result.reshape(shots, stabs, rounds, width), (0, 2, 1, 3))


def solution(mesh):
    placed = (P("shot", "round", "stab", None), P("shot", "round", "stab"), P("round", "stab")) + (P(),) * 16
    return jax.shard_map(
        functools.partial(body, mesh.shape["stab"], mesh.shape["round"]),
        mesh=mesh,
        in_specs=placed,
        out_specs=P("shot", "round", "stab", None),
        check_vma=False,
    )
```

```python
import functools
import math

import jax
import jax.numpy as jnp
from jax import lax
from jax.experimental import pallas as pl
from jax.experimental.pallas import tpu as pltpu
from jax.sharding import PartitionSpec as P

HD = 32
LANES = 128
GROUP = 4
INPUTS = 19
ARRIVALS = ((0, 1, 2, 3), (4, 5, 6, 7), (8, 9, 10, 11), (12, 13), (14, 15))
COUNTS = (128, 256, 256)
MESH = pl.DeviceIdType.MESH
F32 = jnp.float32
BF16 = jnp.bfloat16


def dot(left, right):
    return jnp.dot(left, right, preferred_element_type=F32)


def dot_t(left, right):
    return lax.dot_general(left, right, (((1,), (1,)), ((), ())), preferred_element_type=F32)


def norm_rows(values, gain):
    scale = lax.rsqrt(jnp.mean(values * values, axis=-1, keepdims=True) + 1e-05)
    return values * scale * gain


def row(ref):
    return ref[...].astype(F32).reshape(1, -1)


def pack(rows):
    return jnp.concatenate([rows[:, :LANES], rows[:, LANES:]], axis=0).astype(BF16)


def unpack(message):
    wide = message.astype(F32)
    half = wide.shape[0] // 2
    return jnp.concatenate([wide[:half], wide[half:]], axis=1)


def hop(slot):
    return (slot + 1) // 2 if slot % 2 else -(slot // 2)


def kernel(parts, blocks, *refs):
    sources, refs = refs[:INPUTS], refs[INPUTS:]
    out_ref, refs = refs[0], refs[1:]
    operands, refs = refs[:INPUTS], refs[INPUTS:]
    run(parts, blocks, sources, out_ref, operands, *refs)


def run(
    parts,
    blocks,
    sources,
    out_ref,
    operands,
    wide_ref,
    small_ref,
    start_ref,
    send1,
    recv1,
    q_ref,
    k_ref,
    v_ref,
    n_ref,
    turned_ref,
    across_ref,
    mixed_ref,
    send2,
    recv2,
    after_ref,
    decay_ref,
    drive_ref,
    send3,
    recv3,
    send4,
    recv4,
    send1_sem,
    recv1_sem,
    send2_sem,
    recv2_sem,
    send3_sem,
    recv3_sem,
    send4_sem,
    recv4_sem,
    load_sem,
):
    (states_ref, bits_ref, coords_ref, table_ref, flip_ref, gain_attn_ref, wq_ref, wk_ref, wv_ref, wo_ref) = operands[:10]
    (gain_rec_ref, wd_ref, bias_ref, wi_ref, wr_ref, gain_mlp_ref, wg_ref, wu_ref, wdown_ref) = operands[10:]
    shots, rounds, stabs = bits_ref.shape
    width = states_ref.shape[1]
    rows = start_ref.shape[1]
    coord_rows = table_ref.shape[0]
    heads = width // HD
    gsize = GROUP * rows
    groups = parts // GROUP
    keys = parts * rows
    me = lax.axis_index("stab")
    block = lax.axis_index("round")

    def peer(offset):
        return lax.rem(me + (offset + parts), parts)

    def load(index):
        return pltpu.make_async_copy(sources[index], operands[index], load_sem.at[index])

    barrier = pltpu.get_barrier_semaphore()
    for offset in range(1, parts):
        pl.semaphore_signal(barrier, inc=1, device_id={"stab": peer(offset)}, device_id_type=MESH)
    for offset in range(1, blocks):
        pl.semaphore_signal(
            barrier, inc=1, device_id={"round": lax.rem(block + offset, blocks)}, device_id_type=MESH
        )

    for index in range(INPUTS):
        load(index).start()

    for index in range(6):
        load(index).wait()
    for half in range(2):
        wide_ref[half] = states_ref[:, half * LANES : (half + 1) * LANES].astype(F32)
    small_ref[...] = jnp.zeros_like(small_ref)
    small_ref[0:rounds, 0:stabs] = coords_ref[...].astype(F32)
    for shot in range(shots):
        first = rounds * (1 + shot)
        small_ref[first : first + rounds, 0:stabs] = bits_ref[shot].astype(F32)
    turned = jnp.transpose(small_ref[...])
    small_ref[...] = turned
    small_ref[stabs : stabs + 1, :] = small_ref[stabs - 1 : stabs, :]
    flip = row(flip_ref)
    gain_attn = row(gain_attn_ref)
    spot = lax.broadcasted_iota(jnp.int32, (rows, coord_rows), 1).astype(F32)
    for pair in range(rounds // 2):
        picks = []
        for t in (2 * pair, 2 * pair + 1):
            picks.append(jnp.where(small_ref[0:rows, t : t + 1] == spot, 1.0, 0.0))
        base = dot(jnp.concatenate(picks, axis=0).astype(BF16), table_ref[...])
        for half in range(2):
            t = 2 * pair + half
            for shot in range(shots):
                item = shot * rounds + t
                lane = rounds * (1 + shot) + t
                where = pl.ds(shot * stabs * rounds + t, stabs, stride=rounds)
                own = jnp.concatenate([wide_ref[0, where, :], wide_ref[1, where, :]], axis=1)
                start_ref[item, 0:stabs, :] = own
                start_ref[item, stabs : stabs + 1, :] = own[stabs - 1 : stabs, :]
                sign = 2.0 * small_ref[0:rows, lane : lane + 1] - 1.0
                start = start_ref[item] + base[half * rows : (half + 1) * rows] + sign * flip
                start_ref[item] = start
                send1[item] = pack(norm_rows(start, gain_attn))

    pl.semaphore_wait(barrier, parts - 1 + blocks - 1)

    def copy1(slot):
        offset = hop(slot)
        back = slot if slot in (0, parts - 1) else (slot + 1 if slot % 2 else slot - 1)
        return pltpu.make_async_remote_copy(
            src_ref=send1.at[peer(offset)],
            dst_ref=recv1.at[back],
            send_sem=send1_sem.at[slot],
            recv_sem=recv1_sem.at[back],
            device_id={"stab": peer(offset)},
            device_id_type=MESH,
        )

    for slot in range(1, parts):
        copy1(slot).start()
    recv1[0] = send1[me]

    for index in range(6, INPUTS):
        load(index).wait()
    turned_ref[...] = jnp.transpose(wv_ref[...].astype(F32)).astype(BF16)
    for slots in ARRIVALS:
        pieces = []
        for slot in slots:
            if slot:
                pltpu.make_async_remote_copy(
                    src_ref=send1.at[0],
                    dst_ref=recv1.at[slot],
                    send_sem=send1_sem.at[slot],
                    recv_sem=recv1_sem.at[slot],
                    device_id={"stab": peer(1)},
                    device_id_type=MESH,
                ).wait_recv()
            pieces.append(unpack(recv1[slot]))
        normed = jnp.concatenate(pieces, axis=0).astype(BF16)
        where = slice(slots[0] * rows, (slots[-1] + 1) * rows)
        q_ref[where, :] = dot(normed, wq_ref[...]).astype(BF16)
        k_ref[where, :] = dot(normed, wk_ref[...]).astype(BF16)
        n_ref[where, :] = normed
    real = lax.rem(lax.broadcasted_iota(jnp.int32, (1, keys), 1), rows) < stabs
    values = jnp.where(real, dot_t(turned_ref[...], n_ref[...]), 0.0)
    ones = jnp.where(real, jnp.ones((v_ref.shape[1] - 2 * HD, keys), F32), 0.0).astype(BF16)
    for pair in range(heads // 2):
        v_ref[pair, 0 : 2 * HD, :] = values[2 * HD * pair : 2 * HD * (pair + 1)].astype(BF16)
        v_ref[pair, 2 * HD :, :] = ones

    def copy2(slot, target):
        return pltpu.make_async_remote_copy(
            src_ref=send2.at[slot],
            dst_ref=recv2.at[me],
            send_sem=send2_sem.at[slot],
            recv_sem=recv2_sem.at[me],
            device_id={"stab": target},
            device_id_type=MESH,
        )

    scale = HD ** (-0.5) * math.log2(math.e)
    done = parts
    last = keys
    for count in COUNTS:
        first = last - count
        query = q_ref[first:last, :].astype(F32)
        head_of = lax.broadcasted_iota(jnp.int32, (count, width), 1) // HD
        spread = [jnp.where(head_of == head, query, 0.0) for head in range(heads)]
        scores = dot_t(k_ref[...], jnp.concatenate(spread, axis=0).astype(BF16))
        peak = jnp.max(scores, axis=0, keepdims=True)
        weights = jnp.exp2((scores - peak) * scale).astype(BF16)
        for head in range(0, heads, 2):
            both = dot(v_ref[head // 2], weights[:, head * count : (head + 2) * count])
            for index in range(2):
                piece = both[:, index * count : (index + 1) * count]
                across_ref[(head + index) * HD : (head + index + 1) * HD, 0:count] = (
                    piece[index * HD : (index + 1) * HD] / piece[2 * HD : 2 * HD + 1]
                )
        mixed_ref[first:last, :] = jnp.transpose(across_ref[:, 0:count])
        while done > 0 and (done - 1) * rows >= first:
            done -= 1
            send2[done] = pack(mixed_ref[done * rows : (done + 1) * rows, :])
            if done:
                copy2(done, peer(hop(done))).start()
        last = first
    recv2[me] = send2[0]

    gain_rec = row(gain_rec_ref)
    for group in range(groups - 1, -1, -1):
        pieces, starts = [], []
        for slot in range(group * GROUP, (group + 1) * GROUP):
            item = peer(hop(slot))
            if slot:
                pltpu.make_async_remote_copy(
                    src_ref=send2.at[0],
                    dst_ref=recv2.at[item],
                    send_sem=send2_sem.at[slot],
                    recv_sem=recv2_sem.at[item],
                    device_id={"stab": peer(1)},
                    device_id_type=MESH,
                ).wait_recv()
            pieces.append(unpack(recv2[item]))
            starts.append(start_ref[item])
        mixed = jnp.concatenate(pieces, axis=0).astype(BF16)
        after = jnp.concatenate(starts, axis=0) + dot(mixed, wo_ref[...])
        rec_in = norm_rows(after, gain_rec).astype(BF16)
        decay = jax.nn.sigmoid(dot(rec_in, wd_ref[...]) + row(bias_ref))
        drive = (1.0 - decay) * dot(rec_in, wi_ref[...])
        for index in range(GROUP):
            item = peer(hop(group * GROUP + index))
            part = slice(index * rows, (index + 1) * rows)
            after_ref[item] = after[part]
            decay_ref[item] = decay[part]
            drive_ref[item] = drive[part]

    chunks = 2 * shots
    step = blocks // chunks
    shift = lax.rem(lax.axis_index("shot"), step)
    my_chunk = lax.div(block, step)
    owner = lax.rem(block, step) == shift

    def copy3(chunk):
        return pltpu.make_async_remote_copy(
            src_ref=send3.at[chunk],
            dst_ref=recv3.at[block],
            send_sem=send3_sem.at[chunk],
            recv_sem=recv3_sem.at[block],
            device_id={"round": chunk * step + shift},
            device_id_type=MESH,
        )

    def copy4(target):
        return pltpu.make_async_remote_copy(
            src_ref=send4.at[target],
            dst_ref=recv4.at[my_chunk],
            send_sem=send4_sem.at[target],
            recv_sem=recv4_sem.at[my_chunk],
            device_id={"round": target},
            device_id_type=MESH,
        )

    for shot in range(shots):
        state = drive_ref[shot * rounds]
        product = decay_ref[shot * rounds]
        for t in range(1, rounds):
            item = shot * rounds + t
            decay = decay_ref[item]
            state = decay * state + drive_ref[item]
            product = product * decay
            drive_ref[item] = state
            decay_ref[item] = product
        for half in range(2):
            part = slice(half * LANES, (half + 1) * LANES)
            send3[2 * shot + half] = jnp.concatenate([product[:, part], state[:, part]], axis=0).astype(BF16)
            chunk = 2 * shot + half

            @pl.when((block != chunk * step + shift) & (block < blocks - 1))
            def _():
                copy3(chunk).start()

            @pl.when(block == chunk * step + shift)
            def _():
                recv3[block] = send3[chunk]

    @pl.when(owner)
    def _():
        entering = jnp.zeros((rows, LANES), F32)
        below = jnp.zeros((send4.shape[1] - rows, LANES), F32)
        for source in range(blocks):
            send4[source] = jnp.concatenate([entering, below], axis=0).astype(BF16)

            @pl.when(block != source)
            def _():
                copy4(source).start()

            if source == blocks - 1:
                break

            @pl.when(block != source)
            def _():
                pltpu.make_async_remote_copy(
                    src_ref=send3.at[0],
                    dst_ref=recv3.at[source],
                    send_sem=send3_sem.at[0],
                    recv_sem=recv3_sem.at[source],
                    device_id={"round": source},
                    device_id_type=MESH,
                ).wait_recv()

            wide = recv3[source].astype(F32)
            entering = wide[:rows] * entering + wide[rows:]
        recv4[my_chunk] = send4[block]

    gain_mlp = row(gain_mlp_ref)
    for shot in range(shots):
        halves = []
        for chunk in (2 * shot, 2 * shot + 1):

            @pl.when(block != chunk * step + shift)
            def _():
                pltpu.make_async_remote_copy(
                    src_ref=send4.at[0],
                    dst_ref=recv4.at[chunk],
                    send_sem=send4_sem.at[0],
                    recv_sem=recv4_sem.at[chunk],
                    device_id={"round": chunk * step + shift},
                    device_id_type=MESH,
                ).wait_recv()

            halves.append(recv4[chunk].astype(F32)[:rows])
        entering = jnp.concatenate(halves, axis=1)
        items = range(shot * rounds, (shot + 1) * rounds)
        hidden = [drive_ref[item] + decay_ref[item] * entering for item in items]
        after = jnp.concatenate([after_ref[item] for item in items], axis=0)
        after = after + dot(jnp.concatenate(hidden, axis=0).astype(BF16), wr_ref[...])
        ffn_in = norm_rows(after, gain_mlp).astype(BF16)
        inner = (jax.nn.silu(dot(ffn_in, wg_ref[...])) * dot(ffn_in, wu_ref[...])).astype(BF16)
        states = after + dot(inner, wdown_ref[...])
        for t in range(rounds):
            where = pl.ds(shot * stabs * rounds + t, stabs, stride=rounds)
            for half in range(2):
                wide_ref[half, where, :] = states[t * rows : t * rows + stabs, half * LANES : (half + 1) * LANES]
    for half in range(2):
        out_ref[:, half * LANES : (half + 1) * LANES] = wide_ref[half].astype(BF16)

    for slot in range(1, parts):
        copy1(slot).wait_send()
        copy2(slot, peer(1)).wait_send()
    for chunk in range(chunks):

        @pl.when((block != chunk * step + shift) & (block < blocks - 1))
        def _():
            copy3(chunk).wait_send()

    for target in range(blocks):

        @pl.when(owner & (block != target))
        def _():
            copy4(target).wait_send()


def body(parts, blocks, *args):
    states_in = args[0]
    shots, rounds, stabs, width = states_in.shape
    assert shots * rounds == parts and sum(map(len, ARRIVALS)) == parts
    assert sum(COUNTS) == parts * (-(-stabs // 8) * 8)
    assert len(args) == INPUTS
    rows = -(-stabs // 8) * 8
    flat = (jnp.transpose(states_in, (0, 2, 1, 3)).reshape(-1, width),) + args[1:]
    message = (2 * rows, LANES)
    vmem = pl.BlockSpec(memory_space=pltpu.VMEM)
    dma = pltpu.SemaphoreType.DMA
    result = pl.pallas_call(
        functools.partial(kernel, parts, blocks),
        out_shape=pltpu.VMEM(flat[0].shape, BF16),
        in_specs=[pl.BlockSpec(memory_space=pltpu.HBM)] * len(flat),
        out_specs=vmem,
        scratch_shapes=[pltpu.VMEM(arg.shape, arg.dtype) for arg in flat]
        + [
            pltpu.VMEM((2, flat[0].shape[0], LANES), F32),
            pltpu.VMEM((LANES, LANES), F32),
            pltpu.VMEM((parts, rows, width), F32),
            pltpu.VMEM((parts,) + message, BF16),
            pltpu.VMEM((parts,) + message, BF16),
            pltpu.VMEM((parts * rows, width), BF16),
            pltpu.VMEM((parts * rows, width), BF16),
            pltpu.VMEM((width // (2 * HD), 2 * HD + 16, parts * rows), BF16),
            pltpu.VMEM((parts * rows, width), BF16),
            pltpu.VMEM((width, width), BF16),
            pltpu.VMEM((width, max(COUNTS)), F32),
            pltpu.VMEM((parts * rows, width), F32),
            pltpu.VMEM((parts,) + message, BF16),
            pltpu.VMEM((parts,) + message, BF16),
            pltpu.VMEM((parts, rows, width), F32),
            pltpu.VMEM((parts, rows, width), F32),
            pltpu.VMEM((parts, rows, width), F32),
            pltpu.VMEM((2 * shots,) + message, BF16),
            pltpu.VMEM((blocks,) + message, BF16),
            pltpu.VMEM((blocks, -(-rows // 16) * 16, LANES), BF16),
            pltpu.VMEM((2 * shots, -(-rows // 16) * 16, LANES), BF16),
            dma((parts,)),
            dma((parts,)),
            dma((parts,)),
            dma((parts,)),
            dma((2 * shots,)),
            dma((blocks,)),
            dma((blocks,)),
            dma((2 * shots,)),
            dma((INPUTS,)),
        ],
        compiler_params=pltpu.CompilerParams(
            collective_id=0, has_side_effects=True, vmem_limit_bytes=58 * 1024 * 1024
        ),
    )(*flat)
    return jnp.transpose(result.reshape(shots, stabs, rounds, width), (0, 2, 1, 3))


def solution(mesh):
    placed = (P("shot", "round", "stab", None), P("shot", "round", "stab"), P("round", "stab")) + (P(),) * 16
    return jax.shard_map(
        functools.partial(body, mesh.shape["stab"], mesh.shape["round"]),
        mesh=mesh,
        in_specs=placed,
        out_specs=P("shot", "round", "stab", None),
        check_vma=False,
    )
```
